128 devices in a mesh: fsdp: 16 (over y, x_lo, core), seq: 8 (over x_hi, z).
Axes of the slice: x: 4 (x_hi: 2, x_lo: 2; x = x_hi * 2 + x_lo), y: 4, z: 4, core: 2. Of those that a mesh axis runs over, the one named last changes fastest.
Arguments:
- query_raw: bfloat16 [16384, 3072], P(('fsdp', 'seq')), may hold values from -200 to 200
- key_raw: bfloat16 [16384, 3072], P(('fsdp', 'seq')), may hold values from -200 to 200
- value_in: bfloat16 [16384, 3072], P(('fsdp', 'seq')), may hold values from -6 to 6
- query_dot: bfloat16 [16384, 3072], P(('fsdp', 'seq')), may hold values from -6 to 6
- key_dot: bfloat16 [16384, 3072], P(('fsdp', 'seq')), may hold values from -6 to 6
- value_dot: bfloat16 [16384, 3072], P(('fsdp', 'seq')), may hold values from -6 to 6
- gain_query: float32 [3072], replicated, may hold values from 1 to 2
- gain_key: float32 [3072], replicated, may hold values from 1 to 2
- out_weight: bfloat16 [3072, 5120], P(None, 'fsdp'), may hold values from -0.109375 to 0.109375
- gate_table: float32 [64, 5120], replicated, may hold values from 0.5 to 2
- gate_dot_table: float32 [64, 5120], replicated, may hold values from -6 to 6
- time_index: int32 [16], P('fsdp'), may hold values from 0 to 63
Outputs:
- gated_branch: bfloat16 [16384, 5120], P(('fsdp', 'seq'))
- branch_tangent: bfloat16 [16384, 5120], P(('fsdp', 'seq'))
The draws below stay inside these ranges and needn't reach their ends.
All inputs are finite; a program needn't handle non-finite values.
Results may differ from the reference program's by a relative error of at most 0.012.
Values may be sent and summed in bfloat16 or wider, within the bound.
No kernel may reach another device: no remote copies, remote signals or barrier semaphores. Data moves between devices by JAX's collectives and lax.ppermute only.
A program may use at most 128 MiB of HBM per device.

```python
import math
import jax
import jax.numpy as jnp
from jax import lax

D = 5120
HD = 128
STEPS = 64
HEADS = 24
CLIPS = 16
LENGTH = 1024
TOKENS = 16384


def draw_query_raw(key, part):
    key = jax.random.fold_in(key, 1)
    return jax.random.normal(key, (TOKENS, HEADS * HD), jnp.float32).astype(jnp.bfloat16)


def draw_key_raw(key, part):
    key = jax.random.fold_in(key, 2)
    return jax.random.normal(key, (TOKENS, HEADS * HD), jnp.float32).astype(jnp.bfloat16)


def set_ends(drawn, rng, low, high):
    longest = drawn.shape.index(max(drawn.shape))
    spots = []
    for shift in (0, 1):
        where = [jax.random.randint(jax.random.fold_in(rng, axis), (), 0, length) for axis, length in enumerate(drawn.shape)]
        where[longest] = (where[longest] + shift) % drawn.shape[longest]
        spots.append(tuple(where))
    return drawn.at[spots[0]].set(low).at[spots[1]].set(high)


def levels(own_key, extent, shards, smallest, largest):
    def one(dim, parts):
        heights = jax.random.uniform(jax.random.fold_in(jax.random.fold_in(own_key, 6), dim), (parts,), jnp.float32, smallest / len(shards), largest / len(shards))
        return jnp.repeat(jnp.exp(heights), extent[dim] // parts).reshape((-1,) + (1,) * (len(extent) - dim - 1))

    level = one(*shards[0])
    for cut in shards[1:]:
        level = level * one(*cut)
    return level


def normal_values(stream_key, shape, deviation, most, cuts=(), kind=jnp.bfloat16):
    entries = jax.random.normal(stream_key, shape, jnp.float32) * deviation
    if len(cuts) > 0:
        entries = levels(stream_key, shape, cuts, -0.22, 0.18) * entries
    return jnp.clip(entries, min=-most, max=most).astype(kind)


def setup_inputs(seed: int = 0) -> dict:
    streams_of = jax.random.split(jax.random.key(seed), 13)
    query_raw = draw_query_raw(jax.random.fold_in(streams_of[12], 71), 0)
    key_raw = draw_key_raw(jax.random.fold_in(streams_of[12], 71), 0)
    value_in = normal_values(streams_of[2], (TOKENS, HEADS * HD), 1.0, 6.0, ((0, 128),))
    query_dot = normal_values(streams_of[3], (TOKENS, HEADS * HD), 1.0, 6.0, ((0, 128),))
    key_dot = normal_values(streams_of[4], (TOKENS, HEADS * HD), 1.0, 6.0, ((0, 128),))
    value_dot = normal_values(streams_of[5], (TOKENS, HEADS * HD), 1.0, 6.0, ((0, 128),))
    gain_query = jnp.clip(jnp.exp(jax.random.uniform(streams_of[6], (HEADS * HD,), jnp.float32, math.log(1.0), math.log(2.0))), 1.0, 2.0)
    gain_key = jnp.clip(jnp.exp(jax.random.uniform(streams_of[7], (HEADS * HD,), jnp.float32, math.log(1.0), math.log(2.0))), 1.0, 2.0)
    out_weight = normal_values(streams_of[8], (HEADS * HD, D), (HEADS * HD) ** -0.5, 0.109375, ((1, 16),))
    gate_table = jnp.clip(jax.random.uniform(streams_of[9], (STEPS, D), jnp.float32, 0.5, 2.0), 0.5, 2.0)
    gate_dot_table = normal_values(streams_of[10], (STEPS, D), 1.0, 6.0, (), jnp.float32)
    time_index = set_ends(jax.random.randint(streams_of[11], (CLIPS,), 0, STEPS), jax.random.fold_in(streams_of[11], 1), 0, STEPS - 1).astype(jnp.int32)
    return {"query_raw": query_raw, "key_raw": key_raw, "value_in": value_in, "query_dot": query_dot, "key_dot": key_dot, "value_dot": value_dot, "gain_query": gain_query, "gain_key": gain_key, "out_weight": out_weight, "gate_table": gate_table, "gate_dot_table": gate_dot_table, "time_index": time_index}


eps = 1e-06

def normalize(raw, raw_dot, gain):
    signal = raw.astype(jnp.float32)
    signal_dot = raw_dot.astype(jnp.float32)
    inverse = lax.rsqrt(lax.optimization_barrier(jnp.mean(signal * signal, axis=-1, keepdims=True)) + eps)
    inner = lax.optimization_barrier(jnp.mean(signal * signal_dot, axis=-1, keepdims=True))
    normed = gain * signal * inverse
    normed_dot = gain * (signal_dot * inverse - signal * inverse ** 3 * inner)
    return (normed.astype(jnp.bfloat16), normed_dot.astype(jnp.bfloat16))

def attention(items):
    query_rows, key_rows, value_rows, query_tan, key_tan, value_tan = [a.astype(jnp.float32) for a in items]
    scale = HD ** (-0.5)
    scores = jnp.einsum('qhd,khd->hqk', query_rows, key_rows) * scale
    scores_dot = (jnp.einsum('qhd,khd->hqk', query_tan, key_rows) + jnp.einsum('qhd,khd->hqk', query_rows, key_tan)) * scale
    row_peak = lax.optimization_barrier(jnp.max(scores, axis=-1, keepdims=True))
    weights = jnp.exp(scores - row_peak)
    prob = weights / lax.optimization_barrier(jnp.sum(weights, axis=-1, keepdims=True))
    prob_dot = prob * (scores_dot - lax.optimization_barrier(jnp.sum(prob * scores_dot, axis=-1, keepdims=True)))
    prob_low = lax.optimization_barrier(prob.astype(jnp.bfloat16)).astype(jnp.float32)
    prob_dot_low = lax.optimization_barrier(prob_dot.astype(jnp.bfloat16)).astype(jnp.float32)
    attn = jnp.einsum('hqk,khd->qhd', prob_low, value_rows)
    attn_dot = jnp.einsum('hqk,khd->qhd', prob_dot_low, value_rows) + jnp.einsum('hqk,khd->qhd', prob_low, value_tan)
    return (attn.astype(jnp.bfloat16), attn_dot.astype(jnp.bfloat16))

def reference(query_raw, key_raw, value_in, query_dot, key_dot, value_dot, gain_query, gain_key, out_weight, gate_table, gate_dot_table, time_index):
    query_hat, query_hat_dot = normalize(query_raw, query_dot, gain_query)
    key_hat, key_hat_dot = normalize(key_raw, key_dot, gain_key)
    stacked = tuple((a.reshape(CLIPS, LENGTH, HEADS, HD) for a in (query_hat, key_hat, value_in, query_hat_dot, key_hat_dot, value_dot)))
    attn, attn_dot = lax.map(attention, stacked)
    attn = attn.reshape(TOKENS, HEADS * HD)
    attn_dot = attn_dot.reshape(TOKENS, HEADS * HD)
    proj = jnp.dot(attn, out_weight, preferred_element_type=jnp.float32).reshape(CLIPS, LENGTH, D)
    proj_dot = jnp.dot(attn_dot, out_weight, preferred_element_type=jnp.float32).reshape(CLIPS, LENGTH, D)
    gate = gate_table[time_index][:, None, :]
    gate_dot = gate_dot_table[time_index][:, None, :]
    gated_branch = (gate * proj).astype(jnp.bfloat16).reshape(TOKENS, D)
    branch_tangent = (gate_dot * proj + gate * proj_dot).astype(jnp.bfloat16).reshape(TOKENS, D)
    return (gated_branch, branch_tangent)
```

```python
import functools
import math

import jax
import jax.numpy as jnp
from jax import lax
from jax.experimental import pallas as pl
from jax.experimental.pallas import tpu as pltpu
from jax.sharding import PartitionSpec as P

HD = 128
EPS = 1e-06
F32 = jnp.float32
BF16 = jnp.bfloat16
MIB = 1 << 20
VMEM_ALL = 60 * MIB
PIECE = 320
NO_COST = pl.CostEstimate(flops=0, bytes_accessed=0, transcendentals=0)

NY, NXL, NC, NXH, NZ = 4, 2, 2, 2, 4
NX = NXL * NXH


def place(y, x, core, z):
    x_hi, x_lo = divmod(x % NX, NXL)
    return (((y % NY) * NXL + x_lo) * NC + core) * (NXH * NZ) + x_hi * NZ + z


def chips():
    return [(y, x, z) for y in range(NY) for x in range(NX) for z in range(NZ)]


def along_y(step):
    return [(place(y, x, c, z), place(y + step, x, c, z)) for y, x, z in chips() for c in range(NC)]


def core_swap():
    return [(place(y, x, c, z), place(y, x, 1 - c, z)) for y, x, z in chips() for c in range(NC)]


def beside():
    return [(place(y, x, c, z), place(y, x + 1 - 2 * c, c, z)) for y, x, z in chips() for c in range(NC)]


def move(a, perm):
    return lax.ppermute(a, ("fsdp", "seq"), perm)


def norm_body(q_ref, qd_ref, k_ref, kd_ref, v_ref, vd_ref, gq_ref, gk_ref, *out_refs):
    def normed(raw_ref, dot_ref, gain_ref):
        signal = raw_ref[...].astype(F32)
        signal_dot = dot_ref[...].astype(F32)
        gain = gain_ref[...]
        inverse = lax.rsqrt(jnp.mean(signal * signal, axis=-1, keepdims=True) + EPS)
        inner = jnp.mean(signal * signal_dot, axis=-1, keepdims=True)
        hat = gain * signal * inverse
        hat_dot = gain * (signal_dot * inverse - signal * (inverse * inverse * inverse * inner))
        return hat.astype(BF16), hat_dot.astype(BF16)

    groups = out_refs[0].shape[0]
    counts = [ref.shape[2] // (6 * HD) for ref in out_refs]
    heads = sum(counts)
    target = [(ref, j) for ref, count in zip(out_refs, counts) for j in range(count)]
    q, qd = normed(q_ref, qd_ref, gq_ref)
    k, kd = normed(k_ref, kd_ref, gk_ref)
    pieces = (qd, q, k, kd, v_ref[...], vd_ref[...])
    for g in range(groups):
        for h in range(heads):
            src = (g * heads + h) * HD
            ref, j = target[h]
            for i, piece in enumerate(pieces):
                dst = (6 * j + i) * HD
                ref[g, :, dst : dst + HD] = piece[:, src : src + HD]


def norm_pack(q, qd, k, kd, v, vd, gq, gk, groups, counts):
    tokens, width = q.shape
    rows = 64
    wide = pl.BlockSpec((rows, width), lambda i: (i, 0))
    gain = pl.BlockSpec((1, width), lambda i: (0, 0))
    return pl.pallas_call(
        norm_body,
        grid=(tokens // rows,),
        in_specs=[wide] * 6 + [gain] * 2,
        out_specs=[pl.BlockSpec((groups, rows, n * 6 * HD), lambda i: (0, i, 0)) for n in counts],
        out_shape=[jax.ShapeDtypeStruct((groups, tokens, n * 6 * HD), BF16) for n in counts],
        compiler_params=pltpu.CompilerParams(vmem_limit_bytes=VMEM_ALL),
        cost_estimate=NO_COST,
        name="norm_pack",
    )(q, qd, k, kd, v, vd, gq.reshape(1, width), gk.reshape(1, width))


NT = (((1,), (1,)), ((), ()))
NN = (((1,), (0,)), ((), ()))


def attn_body(in_ref, *refs):
    out_ref = refs[-1]
    groups, tokens, _ = in_ref.shape
    length = groups * tokens
    blocks = 4
    rows = blocks * tokens
    scale = HD**-0.5

    def columns(first, count):
        return in_ref[:, :, first * HD : (first + count) * HD].reshape(length, count * HD)

    k, kk = columns(2, 1), columns(2, 2)
    v, vv = columns(4, 1), columns(4, 2)
    for b in range(0, groups, blocks):
        both = in_ref[b : b + blocks, :, 0 : 2 * HD].reshape(rows, 2 * HD)
        q = in_ref[b : b + blocks, :, HD : 2 * HD].reshape(rows, HD)
        s = lax.dot_general(q, k, NT, preferred_element_type=F32)
        sd = lax.dot_general(both, kk, NT, preferred_element_type=F32)
        peak = jnp.max(s, axis=-1, keepdims=True)
        w = jnp.exp2((s - peak) * (scale * math.log2(math.e)))
        inv = 1.0 / jnp.sum(w, axis=-1, keepdims=True)
        mean = jnp.sum(w * sd, axis=-1, keepdims=True) * inv
        w_dot = (w * (sd - mean)).astype(BF16)
        first = lax.dot_general(w.astype(BF16), vv, NN, preferred_element_type=F32)
        second = lax.dot_general(w_dot, v, NN, preferred_element_type=F32)
        attn = (first[:, :HD] * inv).astype(BF16)
        attn_dot = ((second * scale + first[:, HD:]) * inv).astype(BF16)
        out_ref[b : b + blocks, :, 0:HD] = attn.reshape(blocks, tokens, HD)
        out_ref[b : b + blocks, :, HD : 2 * HD] = attn_dot.reshape(blocks, tokens, HD)


def attend(packed, first, heads, earlier=None):
    groups, tokens, width = packed.shape
    return pl.pallas_call(
        attn_body,
        grid=(width // (6 * HD),),
        in_specs=[pl.BlockSpec((groups, tokens, 6 * HD), lambda h: (0, 0, h))]
        + ([] if earlier is None else [pl.BlockSpec(memory_space=pl.ANY)]),
        out_specs=pl.BlockSpec((groups, tokens, 2 * HD), lambda h: (0, 0, first + h)),
        out_shape=jax.ShapeDtypeStruct((groups, tokens, heads * 2 * HD), BF16),
        input_output_aliases={} if earlier is None else {1: 0},
        compiler_params=pltpu.CompilerParams(vmem_limit_bytes=VMEM_ALL),
        cost_estimate=NO_COST,
        name="attend",
    )(packed, *(() if earlier is None else (earlier,)))


def gates_body(info_ref, gate_hbm, gate_dot_hbm, out_ref, wide, sem):
    copies = []
    for who in range(2):
        row = pl.multiple_of(info_ref[who] // 8 * 8, 8)
        for t, table in enumerate((gate_hbm, gate_dot_hbm)):
            copies.append(pltpu.make_async_copy(table.at[pl.ds(row, 8), :], wide.at[who, t], sem.at[who, t]))
    for c in copies:
        c.start()
    for c in copies:
        c.wait()
    for who in range(2):
        for t in range(2):
            out_ref[2 * who + t : 2 * who + t + 1] = wide[who, t, pl.ds(info_ref[who] % 8, 1), :]


def pick_gates(times, gate_table, gate_dot_table):
    width = gate_table.shape[1]
    hbm = pl.BlockSpec(memory_space=pltpu.HBM)
    return pl.pallas_call(
        gates_body,
        in_specs=[pl.BlockSpec(memory_space=pltpu.SMEM), hbm, hbm],
        out_specs=pl.BlockSpec(memory_space=pltpu.VMEM),
        out_shape=jax.ShapeDtypeStruct((4, width), F32),
        scratch_shapes=[pltpu.VMEM((2, 2, 8, width), F32), pltpu.SemaphoreType.DMA((2, 2))],
        compiler_params=pltpu.CompilerParams(vmem_limit_bytes=VMEM_ALL),
        cost_estimate=NO_COST,
        name="pick_gates",
    )(times, gate_table, gate_dot_table)


def gates_body(info_ref, gate_hbm, gate_dot_hbm, out_ref, wide, sem):
    copies = []
    for who in range(2):
        row = pl.multiple_of(info_ref[who] // 8 * 8, 8)
        for t, table in enumerate((gate_hbm, gate_dot_hbm)):
            copies.append(pltpu.make_async_copy(table.at[pl.ds(row, 8), :], wide.at[who, t], sem.at[who, t]))
    for c in copies:
        c.start()
    for c in copies:
        c.wait()
    for who in range(2):
        for t in range(2):
            out_ref[2 * who + t : 2 * who + t + 1] = wide[who, t, pl.ds(info_ref[who] % 8, 1), :]


def pick_gates(times, gate_table, gate_dot_table):
    width = gate_table.shape[1]
    hbm = pl.BlockSpec(memory_space=pltpu.HBM)
    return pl.pallas_call(
        gates_body,
        in_specs=[pl.BlockSpec(memory_space=pltpu.SMEM), hbm, hbm],
        out_specs=pl.BlockSpec(memory_space=pltpu.VMEM),
        out_shape=jax.ShapeDtypeStruct((4, width), F32),
        scratch_shapes=[pltpu.VMEM((2, 2, 8, width), F32), pltpu.SemaphoreType.DMA((2, 2))],
        compiler_params=pltpu.CompilerParams(vmem_limit_bytes=VMEM_ALL),
        cost_estimate=NO_COST,
        name="pick_gates",
    )(times, gate_table, gate_dot_table)


def round_up(n, unit):
    return -(-n // unit) * unit


def project_body(n, first, info_ref, gates_ref, own_ref, peer_ref, *rest):
    weights = rest[:n]
    mine_ref, send_ref = rest[n : n + 2]
    x, w, w_sem = rest[n + 2 :]
    groups, tokens, _ = own_ref.shape
    heads = own_ref.shape[2] // (2 * HD)

    at, ends, w_copies = 0, [], []
    for i, weight in enumerate(weights):
        rows = weight.shape[0]
        w_copies.append(pltpu.make_async_copy(weight, w.at[pl.ds(at, rows), :], w_sem.at[i]))
        at += rows
        ends.append(at)
    for c in w_copies:
        c.start()

    pieces = ends[-1] // PIECE

    def gate_rows(line):
        parts = []
        for i in range(pieces):
            column = info_ref[first + i] * PIECE
            base = pl.multiple_of(column // HD * HD, HD)
            wide = gates_ref[line : line + 1, pl.ds(base, 3 * HD)]
            parts.append(jnp.where(column % HD != 0, wide[:, HD // 2 : HD // 2 + PIECE], wide[:, :PIECE]))
        return jnp.concatenate(parts, axis=1)

    lines = [gate_rows(line) for line in range(4)]
    for who, ref in enumerate((own_ref, peer_ref)):
        for g in range(groups):
            for h in range(heads):
                at = (g * heads + h) * HD
                for t in range(2):
                    row = (2 * who + t) * tokens
                    src = (2 * h + t) * HD
                    x[row : row + tokens, at : at + HD] = ref[g, :, src : src + HD]
    for c in w_copies:
        c.wait()
    y = lax.dot_general(x[...], w[...], NT, preferred_element_type=F32)
    for who, ref in enumerate((mine_ref, send_ref)):
        gate, gate_dot = lines[2 * who], lines[2 * who + 1]
        primal = y[2 * who * tokens : (2 * who + 1) * tokens]
        tangent = y[(2 * who + 1) * tokens : (2 * who + 2) * tokens]
        ref[0] = (gate * primal).astype(BF16)
        ref[1] = (gate_dot * primal + gate * tangent).astype(BF16)


def project(info, first, own, peer, gates, weights):
    groups, tokens, _ = own.shape
    n = len(weights)
    total = sum(a.shape[0] for a in weights)
    depth = weights[0].shape[1]
    hbm = pl.BlockSpec(memory_space=pltpu.HBM)
    vmem = pl.BlockSpec(memory_space=pltpu.VMEM)
    half = jax.ShapeDtypeStruct((2, tokens, total), BF16)
    return pl.pallas_call(
        functools.partial(project_body, n, first),
        in_specs=[pl.BlockSpec(memory_space=pltpu.SMEM)] + [vmem] * 3 + [hbm] * n,
        out_specs=[vmem, vmem],
        out_shape=[half, half],
        scratch_shapes=[
            pltpu.VMEM((4 * tokens, depth), BF16),
            pltpu.VMEM((total, depth), BF16),
            pltpu.SemaphoreType.DMA((n,)),
        ],
        compiler_params=pltpu.CompilerParams(vmem_limit_bytes=36 * MIB),
        cost_estimate=NO_COST,
        name="project",
    )(info, gates, own, peer, *weights)


def merge_body(spots, info_ref, *refs):
    parts = (len(refs) - 2) // 2
    out_refs = refs[2 * parts :]
    first = info_ref[8] == 0
    for i, (part, at) in enumerate(spots):
        own_ref, got_ref = refs[part], refs[parts + part]
        cols = 2 * PIECE
        column = pl.multiple_of(info_ref[9 + i] * cols, cols)
        here = slice(at * PIECE, (at + 1) * PIECE)
        for t in range(2):
            own, got = own_ref[t, :, here], got_ref[t, :, here]
            low = jnp.where(first, own, got)
            high = jnp.where(first, got, own)
            out_refs[t][:, pl.ds(column, cols)] = jnp.concatenate([low, high], axis=1)


def merge(info, spots, owns, gots, width):
    tokens = owns[0].shape[1]
    vmem = pl.BlockSpec(memory_space=pltpu.VMEM)
    out = jax.ShapeDtypeStruct((tokens, width), BF16)
    return pl.pallas_call(
        functools.partial(merge_body, spots),
        in_specs=[pl.BlockSpec(memory_space=pltpu.SMEM)] + [vmem] * (2 * len(owns)),
        out_specs=[vmem, vmem],
        out_shape=[out, out],
        compiler_params=pltpu.CompilerParams(vmem_limit_bytes=12 * MIB),
        cost_estimate=NO_COST,
        name="merge",
    )(info, *owns, *gots)


def local(
    query_raw,
    key_raw,
    value_in,
    query_dot,
    key_dot,
    value_dot,
    gain_query,
    gain_key,
    out_weight,
    gate_table,
    gate_dot_table,
    time_index,
):
    groups = lax.axis_size("seq")
    fsdp = lax.axis_index("fsdp")
    core = fsdp % NC
    x_lo = fsdp // NC % NXL
    y = fsdp // (NC * NXL)
    up, down, swap = along_y(1), along_y(-1), core_swap()

    def exchange(a):
        return lax.all_to_all(a, "seq", split_axis=0, concat_axis=0, tiled=True)

    other = 1 - x_lo
    steps = (0, -1, 1, 2)
    block = [(y + step) % NY * NXL + low for low in (x_lo, other) for step in steps]
    source = [index * NC + core for index in block]
    info = jnp.stack([jnp.asarray(v, jnp.int32) for v in (*source, core, *block)])

    weight = out_weight.T
    half = PIECE // 2
    near = move(weight, beside())
    w1 = weight[:half]
    a1 = move(w1, up)
    b1 = move(w1, down)
    peer_time = move(time_index, swap)
    (packed,) = norm_pack(
        query_raw, query_dot, key_raw, key_dot, value_in, value_dot, gain_query, gain_key, groups, (3,)
    )
    times = jnp.concatenate([time_index, peer_time])
    packed, weight, near, a1, b1, times, info = lax.optimization_barrier(
        (packed, weight, near, a1, b1, times, info)
    )

    received = exchange(packed)
    w2 = weight[half:]
    a2 = move(w2, up)
    b2 = move(w2, down)
    c1 = move(a1, up)
    c2 = move(b2, down)
    near_a = move(near, up)
    near_b = move(near, down)
    received, a2, b2, c1, c2 = lax.optimization_barrier((received, a2, b2, c1, c2))

    attn = attend(received, 0, 3)
    own = exchange(attn)
    gates = pick_gates(times, gate_table, gate_dot_table)
    own, near_a, near_b, gates, c2 = lax.optimization_barrier((own, near_a, near_b, gates, c2))

    peer = move(own, swap)
    near_c1 = move(near_a[: half // 2], up)
    near_c2 = move(near_b[half // 2 : half], down)
    near_c3 = move(c2, beside())

    mine_a, sent_a = project(info, 0, own, peer, gates, (weight, a1, a2, b1, b2, c1, c2))
    got_a = move(sent_a, swap)
    mine_b, sent_b = project(info, 4, own, peer, gates, (near, near_a, near_b, near_c1, near_c2, near_c3))
    got_b = move(sent_b, swap)
    spots = [(part, i) for part in range(2) for i in range(4)]
    return tuple(merge(info, spots, (mine_a, mine_b), (got_a, got_b), gate_table.shape[1]))


def solution(mesh):
    return jax.shard_map(
        local,
        mesh=mesh,
        in_specs=(
            P(("fsdp", "seq"), None),
            P(("fsdp", "seq"), None),
            P(("fsdp", "seq"), None),
            P(("fsdp", "seq"), None),
            P(("fsdp", "seq"), None),
            P(("fsdp", "seq"), None),
            P(),
            P(),
            P(None, "fsdp"),
            P(),
            P(),
            P("fsdp"),
        ),
        out_specs=(P(("fsdp", "seq"), None), P(("fsdp", "seq"), None)),
        check_vma=False,
    )
```

```python
import functools
import math

import jax
import jax.numpy as jnp
from jax import lax
from jax.experimental import pallas as pl
from jax.experimental.pallas import tpu as pltpu
from jax.sharding import PartitionSpec as P

HD = 128
EPS = 1e-06
F32 = jnp.float32
BF16 = jnp.bfloat16
MIB = 1 << 20
VMEM_ALL = 60 * MIB
PIECE = 320
NO_COST = pl.CostEstimate(flops=0, bytes_accessed=0, transcendentals=0)

NY, NXL, NC, NXH, NZ = 4, 2, 2, 2, 4
NX = NXL * NXH


def place(y, x, core, z):
    x_hi, x_lo = divmod(x % NX, NXL)
    return (((y % NY) * NXL + x_lo) * NC + core) * (NXH * NZ) + x_hi * NZ + z


def chips():
    return [(y, x, z) for y in range(NY) for x in range(NX) for z in range(NZ)]


def along_y(step):
    return [(place(y, x, c, z), place(y + step, x, c, z)) for y, x, z in chips() for c in range(NC)]


def core_swap():
    return [(place(y, x, c, z), place(y, x, 1 - c, z)) for y, x, z in chips() for c in range(NC)]


def beside():
    return [(place(y, x, c, z), place(y, x + 1 - 2 * c, c, z)) for y, x, z in chips() for c in range(NC)]


def move(a, perm):
    return lax.ppermute(a, ("fsdp", "seq"), perm)


def norm_body(q_ref, qd_ref, k_ref, kd_ref, v_ref, vd_ref, gq_ref, gk_ref, *out_refs):
    def normed(raw_ref, dot_ref, gain_ref):
        signal = raw_ref[...].astype(F32)
        signal_dot = dot_ref[...].astype(F32)
        gain = gain_ref[...]
        inverse = lax.rsqrt(jnp.mean(signal * signal, axis=-1, keepdims=True) + EPS)
        inner = jnp.mean(signal * signal_dot, axis=-1, keepdims=True)
        hat = gain * signal * inverse
        hat_dot = gain * (signal_dot * inverse - signal * (inverse * inverse * inverse * inner))
        return hat.astype(BF16), hat_dot.astype(BF16)

    groups = out_refs[0].shape[0]
    counts = [ref.shape[2] // (6 * HD) for ref in out_refs]
    heads = sum(counts)
    target = [(ref, j) for ref, count in zip(out_refs, counts) for j in range(count)]
    q, qd = normed(q_ref, qd_ref, gq_ref)
    k, kd = normed(k_ref, kd_ref, gk_ref)
    pieces = (qd, q, k, kd, v_ref[...], vd_ref[...])
    for g in range(groups):
        for h in range(heads):
            src = (g * heads + h) * HD
            ref, j = target[h]
            for i, piece in enumerate(pieces):
                dst = (6 * j + i) * HD
                ref[g, :, dst : dst + HD] = piece[:, src : src + HD]


def norm_pack(q, qd, k, kd, v, vd, gq, gk, groups, counts):
    tokens, width = q.shape
    rows = 64
    wide = pl.BlockSpec((rows, width), lambda i: (i, 0))
    gain = pl.BlockSpec((1, width), lambda i: (0, 0))
    return pl.pallas_call(
        norm_body,
        grid=(tokens // rows,),
        in_specs=[wide] * 6 + [gain] * 2,
        out_specs=[pl.BlockSpec((groups, rows, n * 6 * HD), lambda i: (0, i, 0)) for n in counts],
        out_shape=[jax.ShapeDtypeStruct((groups, tokens, n * 6 * HD), BF16) for n in counts],
        compiler_params=pltpu.CompilerParams(vmem_limit_bytes=VMEM_ALL),
        cost_estimate=NO_COST,
        name="norm_pack",
    )(q, qd, k, kd, v, vd, gq.reshape(1, width), gk.reshape(1, width))


NT = (((1,), (1,)), ((), ()))
NN = (((1,), (0,)), ((), ()))


def attn_body(in_ref, *refs):
    out_ref = refs[-1]
    groups, tokens, _ = in_ref.shape
    length = groups * tokens
    blocks = 4
    rows = blocks * tokens
    scale = HD**-0.5

    def columns(first, count):
        return in_ref[:, :, first * HD : (first + count) * HD].reshape(length, count * HD)

    k, kk = columns(2, 1), columns(2, 2)
    v, vv = columns(4, 1), columns(4, 2)
    for b in range(0, groups, blocks):
        both = in_ref[b : b + blocks, :, 0 : 2 * HD].reshape(rows, 2 * HD)
        q = in_ref[b : b + blocks, :, HD : 2 * HD].reshape(rows, HD)
        s = lax.dot_general(q, k, NT, preferred_element_type=F32)
        sd = lax.dot_general(both, kk, NT, preferred_element_type=F32)
        peak = jnp.max(s, axis=-1, keepdims=True)
        w = jnp.exp2((s - peak) * (scale * math.log2(math.e)))
        inv = 1.0 / jnp.sum(w, axis=-1, keepdims=True)
        mean = jnp.sum(w * sd, axis=-1, keepdims=True) * inv
        w_dot = (w * (sd - mean)).astype(BF16)
        first = lax.dot_general(w.astype(BF16), vv, NN, preferred_element_type=F32)
        second = lax.dot_general(w_dot, v, NN, preferred_element_type=F32)
        attn = (first[:, :HD] * inv).astype(BF16)
        attn_dot = ((second * scale + first[:, HD:]) * inv).astype(BF16)
        out_ref[b : b + blocks, :, 0:HD] = attn.reshape(blocks, tokens, HD)
        out_ref[b : b + blocks, :, HD : 2 * HD] = attn_dot.reshape(blocks, tokens, HD)


def attend(packed, first, heads, earlier=None):
    groups, tokens, width = packed.shape
    return pl.pallas_call(
        attn_body,
        grid=(width // (6 * HD),),
        in_specs=[pl.BlockSpec((groups, tokens, 6 * HD), lambda h: (0, 0, h))]
        + ([] if earlier is None else [pl.BlockSpec(memory_space=pl.ANY)]),
        out_specs=pl.BlockSpec((groups, tokens, 2 * HD), lambda h: (0, 0, first + h)),
        out_shape=jax.ShapeDtypeStruct((groups, tokens, heads * 2 * HD), BF16),
        input_output_aliases={} if earlier is None else {1: 0},
        compiler_params=pltpu.CompilerParams(vmem_limit_bytes=VMEM_ALL),
        cost_estimate=NO_COST,
        name="attend",
    )(packed, *(() if earlier is None else (earlier,)))


def prepare_body(n, info_ref, gate_hbm, gate_dot_hbm, *rest):
    weights = rest[:n]
    gates_ref, w_ref, wide, sem, w_sem = rest[n:]
    copies, at = [], 0
    for who in range(2):
        row = pl.multiple_of(info_ref[who] // 8 * 8, 8)
        for t, table in enumerate((gate_hbm, gate_dot_hbm)):
            copies.append(pltpu.make_async_copy(table.at[pl.ds(row, 8), :], wide.at[who, t], sem.at[who, t]))
    for i, weight in enumerate(weights):
        rows = weight.shape[0]
        copies.append(pltpu.make_async_copy(weight, w_ref.at[pl.ds(at, rows), :], w_sem.at[i]))
        at += rows
    for c in copies:
        c.start()
    for c in copies:
        c.wait()
    for who in range(2):
        for t in range(2):
            gates_ref[2 * who + t : 2 * who + t + 1] = wide[who, t, pl.ds(info_ref[who] % 8, 1), :]


def prepare(times, gate_table, gate_dot_table, weights):
    width = gate_table.shape[1]
    n = len(weights)
    total = sum(a.shape[0] for a in weights)
    anywhere = pl.BlockSpec(memory_space=pl.ANY)
    vmem = pl.BlockSpec(memory_space=pltpu.VMEM)
    return pl.pallas_call(
        functools.partial(prepare_body, n),
        in_specs=[pl.BlockSpec(memory_space=pltpu.SMEM)] + [anywhere] * (2 + n),
        out_specs=[vmem, vmem],
        out_shape=[
            jax.ShapeDtypeStruct((4, width), F32),
            jax.ShapeDtypeStruct((total, weights[0].shape[1]), BF16),
        ],
        scratch_shapes=[
            pltpu.VMEM((2, 2, 8, width), F32),
            pltpu.SemaphoreType.DMA((2, 2)),
            pltpu.SemaphoreType.DMA((n,)),
        ],
        compiler_params=pltpu.CompilerParams(vmem_limit_bytes=36 * MIB),
        cost_estimate=NO_COST,
        name="prepare",
    )(times, gate_table, gate_dot_table, *weights)


def round_up(n, unit):
    return -(-n // unit) * unit


def project_body(n, first, ready_rows, info_ref, gates_ref, own_ref, peer_ref, *rest):
    ready = rest[0] if ready_rows else None
    rest = rest[1:] if ready_rows else rest
    weights = rest[:n]
    mine_ref, send_ref, x, w, w_sem = rest[n:]
    groups, tokens, _ = own_ref.shape
    heads = own_ref.shape[2] // (2 * HD)

    at, w_copies = 0, []
    for i, weight in enumerate(weights):
        rows = weight.shape[0]
        w_copies.append(pltpu.make_async_copy(weight, w.at[pl.ds(at, rows), :], w_sem.at[i]))
        at += rows
    for c in w_copies:
        c.start()

    def gate_rows(line, begin, end):
        parts = []
        for i in range(begin // PIECE, end // PIECE):
            column = info_ref[first + i] * PIECE
            base = pl.multiple_of(column // HD * HD, HD)
            wide = gates_ref[line : line + 1, pl.ds(base, 3 * HD)]
            parts.append(jnp.where(column % HD != 0, wide[:, HD // 2 : HD // 2 + PIECE], wide[:, :PIECE]))
        return jnp.concatenate(parts, axis=1)

    for who, ref in enumerate((own_ref, peer_ref)):
        for g in range(groups):
            for h in range(heads):
                at = (g * heads + h) * HD
                for t in range(2):
                    row = (2 * who + t) * tokens
                    src = (2 * h + t) * HD
                    x[row : row + tokens, at : at + HD] = ref[g, :, src : src + HD]

    def part(weight_ref, begin):
        end = begin + weight_ref.shape[0]
        y = lax.dot_general(x[...], weight_ref[...], NT, preferred_element_type=F32)
        for who, ref in enumerate((mine_ref, send_ref)):
            gate, gate_dot = (gate_rows(2 * who + t, begin, end) for t in range(2))
            primal = y[2 * who * tokens : (2 * who + 1) * tokens]
            tangent = y[(2 * who + 1) * tokens : (2 * who + 2) * tokens]
            ref[0, :, begin:end] = (gate * primal).astype(BF16)
            ref[1, :, begin:end] = (gate_dot * primal + gate * tangent).astype(BF16)

    if ready_rows:
        part(ready, 0)
    for c in w_copies:
        c.wait()
    part(w, ready_rows)


def project(info, first, own, peer, gates, ready, weights):
    groups, tokens, _ = own.shape
    n = len(weights)
    rows = sum(a.shape[0] for a in weights)
    ready_rows = 0 if ready is None else ready.shape[0]
    depth = weights[0].shape[1]
    hbm = pl.BlockSpec(memory_space=pltpu.HBM)
    vmem = pl.BlockSpec(memory_space=pltpu.VMEM)
    half = jax.ShapeDtypeStruct((2, tokens, round_up(ready_rows + rows, HD)), BF16)
    return pl.pallas_call(
        functools.partial(project_body, n, first, ready_rows),
        in_specs=[pl.BlockSpec(memory_space=pltpu.SMEM)] + [vmem] * (3 if ready is None else 4) + [hbm] * n,
        out_specs=[vmem, vmem],
        out_shape=[half, half],
        scratch_shapes=[
            pltpu.VMEM((4 * tokens, depth), BF16),
            pltpu.VMEM((rows, depth), BF16),
            pltpu.SemaphoreType.DMA((n,)),
        ],
        compiler_params=pltpu.CompilerParams(vmem_limit_bytes=36 * MIB),
        cost_estimate=NO_COST,
        name="project",
    )(info, gates, own, peer, *(() if ready is None else (ready,)), *weights)


def merge_body(spots, info_ref, *refs):
    parts = (len(refs) - 2) // 2
    out_refs = refs[2 * parts :]
    first = info_ref[8] == 0
    for i, (part, at) in enumerate(spots):
        own_ref, got_ref = refs[part], refs[parts + part]
        cols = 2 * PIECE
        column = pl.multiple_of(info_ref[9 + i] * cols, cols)
        here = slice(at * PIECE, (at + 1) * PIECE)
        for t in range(2):
            own, got = own_ref[t, :, here], got_ref[t, :, here]
            low = jnp.where(first, own, got)
            high = jnp.where(first, got, own)
            out_refs[t][:, pl.ds(column, cols)] = jnp.concatenate([low, high], axis=1)


def merge(info, spots, owns, gots, width):
    tokens = owns[0].shape[1]
    vmem = pl.BlockSpec(memory_space=pltpu.VMEM)
    out = jax.ShapeDtypeStruct((tokens, width), BF16)
    return pl.pallas_call(
        functools.partial(merge_body, spots),
        in_specs=[pl.BlockSpec(memory_space=pltpu.SMEM)] + [vmem] * (2 * len(owns)),
        out_specs=[vmem, vmem],
        out_shape=[out, out],
        compiler_params=pltpu.CompilerParams(vmem_limit_bytes=12 * MIB),
        cost_estimate=NO_COST,
        name="merge",
    )(info, *owns, *gots)


def local(
    query_raw,
    key_raw,
    value_in,
    query_dot,
    key_dot,
    value_dot,
    gain_query,
    gain_key,
    out_weight,
    gate_table,
    gate_dot_table,
    time_index,
):
    groups = lax.axis_size("seq")
    fsdp = lax.axis_index("fsdp")
    core = fsdp % NC
    x_lo = fsdp // NC % NXL
    y = fsdp // (NC * NXL)
    up, down, swap = along_y(1), along_y(-1), core_swap()

    def exchange(a):
        return lax.all_to_all(a, "seq", split_axis=0, concat_axis=0, tiled=True)

    other = 1 - x_lo
    steps = (0, -1, 1, 2)
    block = [(y + step) % NY * NXL + low for low in (x_lo, other) for step in steps]
    source = [index * NC + core for index in block]
    info = jnp.stack([jnp.asarray(v, jnp.int32) for v in (*source, core, *block)])

    weight = out_weight.T
    half = PIECE // 2
    near = move(weight, beside())
    w1 = weight[:half]
    a1 = move(w1, up)
    b1 = move(w1, down)
    peer_time = move(time_index, swap)
    (packed,) = norm_pack(
        query_raw, query_dot, key_raw, key_dot, value_in, value_dot, gain_query, gain_key, groups, (3,)
    )
    times = jnp.concatenate([time_index, peer_time])
    packed, weight, near, a1, b1, times, info = lax.optimization_barrier(
        (packed, weight, near, a1, b1, times, info)
    )

    received = exchange(packed)
    w2 = weight[half:]
    a2 = move(w2, up)
    b2 = move(w2, down)
    c1 = move(a1, up)
    c2 = move(b2, down)
    near_a = move(near, up)
    near_b = move(near, down)
    received, a2, b2, c1, c2 = lax.optimization_barrier((received, a2, b2, c1, c2))

    attn = attend(received, 0, 3)
    own = exchange(attn)
    gates, here = prepare(times, gate_table, gate_dot_table, (weight, a1, a2, b1, b2, c1, c2))
    own, near_a, near_b, gates, here, c2 = lax.optimization_barrier((own, near_a, near_b, gates, here, c2))

    peer = move(own, swap)
    near_c1 = move(near_a[: half // 2], up)
    near_c2 = move(near_b[half // 2 : half], down)
    near_c3 = move(c2, beside())

    mine_a, sent_a = project(info, 0, own, peer, gates, here, (near, near_a, near_b))
    mine_a, sent_a, near_c1, near_c2, near_c3 = lax.optimization_barrier((mine_a, sent_a, near_c1, near_c2, near_c3))
    got_a = move(sent_a, swap)
    mine_b, sent_b = project(info, 7, own, peer, gates, None, (near_c1, near_c2, near_c3))
    got_b = move(sent_b, swap)
    spots = [(0, i) for i in range(7)] + [(1, 0)]
    return tuple(merge(info, spots, (mine_a, mine_b), (got_a, got_b), gate_table.shape[1]))


def solution(mesh):
    return jax.shard_map(
        local,
        mesh=mesh,
        in_specs=(
            P(("fsdp", "seq"), None),
            P(("fsdp", "seq"), None),
            P(("fsdp", "seq"), None),
            P(("fsdp", "seq"), None),
            P(("fsdp", "seq"), None),
            P(("fsdp", "seq"), None),
            P(),
            P(),
            P(None, "fsdp"),
            P(),
            P(),
            P("fsdp"),
        ),
        out_specs=(P(("fsdp", "seq"), None), P(("fsdp", "seq"), None)),
        check_vma=False,
    )
```

```python
import functools
import math

import jax
import jax.numpy as jnp
from jax import lax
from jax.experimental import pallas as pl
from jax.experimental.pallas import tpu as pltpu
from jax.sharding import PartitionSpec as P

HD = 128
EPS = 1e-06
F32 = jnp.float32
BF16 = jnp.bfloat16
MIB = 1 << 20
VMEM_ALL = 60 * MIB
PIECE = 320
NO_COST = pl.CostEstimate(flops=0, bytes_accessed=0, transcendentals=0)

NY, NXL, NC, NXH, NZ = 4, 2, 2, 2, 4
NX = NXL * NXH


def place(y, x, core, z):
    x_hi, x_lo = divmod(x % NX, NXL)
    return (((y % NY) * NXL + x_lo) * NC + core) * (NXH * NZ) + x_hi * NZ + z


def chips():
    return [(y, x, z) for y in range(NY) for x in range(NX) for z in range(NZ)]


def along_y(step):
    return [(place(y, x, c, z), place(y + step, x, c, z)) for y, x, z in chips() for c in range(NC)]


def core_swap():
    return [(place(y, x, c, z), place(y, x, 1 - c, z)) for y, x, z in chips() for c in range(NC)]


def beside():
    return [(place(y, x, c, z), place(y, x + 1 - 2 * c, c, z)) for y, x, z in chips() for c in range(NC)]


def move(a, perm):
    return lax.ppermute(a, ("fsdp", "seq"), perm)


def norm_body(q_ref, qd_ref, k_ref, kd_ref, v_ref, vd_ref, gq_ref, gk_ref, *out_refs):
    def normed(raw_ref, dot_ref, gain_ref):
        signal = raw_ref[...].astype(F32)
        signal_dot = dot_ref[...].astype(F32)
        gain = gain_ref[...]
        inverse = lax.rsqrt(jnp.mean(signal * signal, axis=-1, keepdims=True) + EPS)
        inner = jnp.mean(signal * signal_dot, axis=-1, keepdims=True)
        hat = gain * signal * inverse
        hat_dot = gain * (signal_dot * inverse - signal * (inverse * inverse * inverse * inner))
        return hat.astype(BF16), hat_dot.astype(BF16)

    groups = out_refs[0].shape[0]
    counts = [ref.shape[2] // (6 * HD) for ref in out_refs]
    heads = sum(counts)
    target = [(ref, j) for ref, count in zip(out_refs, counts) for j in range(count)]
    q, qd = normed(q_ref, qd_ref, gq_ref)
    k, kd = normed(k_ref, kd_ref, gk_ref)
    pieces = (qd, q, k, kd, v_ref[...], vd_ref[...])
    for g in range(groups):
        for h in range(heads):
            src = (g * heads + h) * HD
            ref, j = target[h]
            for i, piece in enumerate(pieces):
                dst = (6 * j + i) * HD
                ref[g, :, dst : dst + HD] = piece[:, src : src + HD]


def norm_pack(q, qd, k, kd, v, vd, gq, gk, groups, counts):
    tokens, width = q.shape
    rows = 64
    wide = pl.BlockSpec((rows, width), lambda i: (i, 0))
    gain = pl.BlockSpec((1, width), lambda i: (0, 0))
    return pl.pallas_call(
        norm_body,
        grid=(tokens // rows,),
        in_specs=[wide] * 6 + [gain] * 2,
        out_specs=[pl.BlockSpec((groups, rows, n * 6 * HD), lambda i: (0, i, 0)) for n in counts],
        out_shape=[jax.ShapeDtypeStruct((groups, tokens, n * 6 * HD), BF16) for n in counts],
        compiler_params=pltpu.CompilerParams(vmem_limit_bytes=VMEM_ALL),
        cost_estimate=NO_COST,
        name="norm_pack",
    )(q, qd, k, kd, v, vd, gq.reshape(1, width), gk.reshape(1, width))


NT = (((1,), (1,)), ((), ()))
NN = (((1,), (0,)), ((), ()))


def attn_body(in_ref, *refs):
    out_ref = refs[-1]
    groups, tokens, _ = in_ref.shape
    length = groups * tokens
    blocks = 8
    rows = blocks * tokens
    scale = HD**-0.5

    def columns(first, count):
        return in_ref[:, :, first * HD : (first + count) * HD].reshape(length, count * HD)

    k, kk = columns(2, 1), columns(2, 2)
    v, vv = columns(4, 1), columns(4, 2)
    for b in range(0, groups, blocks):
        both = in_ref[b : b + blocks, :, 0 : 2 * HD].reshape(rows, 2 * HD)
        q = in_ref[b : b + blocks, :, HD : 2 * HD].reshape(rows, HD)
        s = lax.dot_general(q, k, NT, preferred_element_type=F32)
        sd = lax.dot_general(both, kk, NT, preferred_element_type=F32)
        peak = jnp.max(s, axis=-1, keepdims=True)
        w = jnp.exp2((s - peak) * (scale * math.log2(math.e)))
        inv = 1.0 / jnp.sum(w, axis=-1, keepdims=True)
        mean = jnp.sum(w * sd, axis=-1, keepdims=True) * inv
        w_dot = (w * (sd - mean)).astype(BF16)
        first = lax.dot_general(w.astype(BF16), vv, NN, preferred_element_type=F32)
        second = lax.dot_general(w_dot, v, NN, preferred_element_type=F32)
        attn = (first[:, :HD] * inv).astype(BF16)
        attn_dot = ((second * scale + first[:, HD:]) * inv).astype(BF16)
        out_ref[b : b + blocks, :, 0:HD] = attn.reshape(blocks, tokens, HD)
        out_ref[b : b + blocks, :, HD : 2 * HD] = attn_dot.reshape(blocks, tokens, HD)


def attend(packed, first, heads, earlier=None):
    groups, tokens, width = packed.shape
    return pl.pallas_call(
        attn_body,
        grid=(width // (6 * HD),),
        in_specs=[pl.BlockSpec((groups, tokens, 6 * HD), lambda h: (0, 0, h))]
        + ([] if earlier is None else [pl.BlockSpec(memory_space=pl.ANY)]),
        out_specs=pl.BlockSpec((groups, tokens, 2 * HD), lambda h: (0, 0, first + h)),
        out_shape=jax.ShapeDtypeStruct((groups, tokens, heads * 2 * HD), BF16),
        input_output_aliases={} if earlier is None else {1: 0},
        compiler_params=pltpu.CompilerParams(vmem_limit_bytes=VMEM_ALL),
        cost_estimate=NO_COST,
        name="attend",
    )(packed, *(() if earlier is None else (earlier,)))


def prepare_body(n, times_ref, info_ref, gate_hbm, gate_dot_hbm, *rest):
    weights = rest[:n]
    gates_ref, w_ref, wide, sem, w_sem = rest[n:]
    copies, at = [], 0
    for who in range(2):
        row = pl.multiple_of(times_ref[who] // 8 * 8, 8)
        for t, table in enumerate((gate_hbm, gate_dot_hbm)):
            copies.append(pltpu.make_async_copy(table.at[pl.ds(row, 8), :], wide.at[who, t], sem.at[who, t]))
    for i, weight in enumerate(weights):
        rows = weight.shape[0]
        copies.append(pltpu.make_async_copy(weight, w_ref.at[pl.ds(at, rows), :], w_sem.at[i]))
        at += rows
    for c in copies:
        c.start()
    for c in copies:
        c.wait()
    for who in range(2):
        row = times_ref[who] % 8
        for t in range(2):
            parts = []
            for i in range(gates_ref.shape[1] // PIECE):
                column = info_ref[i] * PIECE
                base = pl.multiple_of(column // HD * HD, HD)
                line = wide[who, t, pl.ds(row, 1), pl.ds(base, 3 * HD)]
                parts.append(jnp.where(column % HD != 0, line[:, HD // 2 : HD // 2 + PIECE], line[:, :PIECE]))
            gates_ref[2 * who + t : 2 * who + t + 1] = jnp.concatenate(parts, axis=1)


def prepare(times, info, gate_table, gate_dot_table, weights):
    width = gate_table.shape[1]
    n = len(weights)
    total = sum(a.shape[0] for a in weights)
    anywhere = pl.BlockSpec(memory_space=pl.ANY)
    vmem = pl.BlockSpec(memory_space=pltpu.VMEM)
    return pl.pallas_call(
        functools.partial(prepare_body, n),
        in_specs=[pl.BlockSpec(memory_space=pltpu.SMEM)] * 2 + [anywhere] * (2 + n),
        out_specs=[vmem, vmem],
        out_shape=[
            jax.ShapeDtypeStruct((4, 8 * PIECE), F32),
            jax.ShapeDtypeStruct((total, weights[0].shape[1]), BF16),
        ],
        scratch_shapes=[
            pltpu.VMEM((2, 2, 8, width), F32),
            pltpu.SemaphoreType.DMA((2, 2)),
            pltpu.SemaphoreType.DMA((n,)),
        ],
        compiler_params=pltpu.CompilerParams(vmem_limit_bytes=VMEM_ALL),
        cost_estimate=NO_COST,
        name="prepare",
    )(times, info, gate_table, gate_dot_table, *weights)


def round_up(n, unit):
    return -(-n // unit) * unit


def project_body(n, first, ready_rows, plan, gates_ref, own_ref, peer_ref, *rest):
    ready = rest[0] if ready_rows else None
    rest = rest[1:] if ready_rows else rest
    weights = rest[:n]
    mine_ref, send_ref, x, w, w_sem = rest[n:]
    groups, tokens, _ = own_ref.shape
    heads = own_ref.shape[2] // (2 * HD)

    at, w_copies = 0, []
    for i, (which, start, rows) in enumerate(plan):
        piece = weights[which].at[pl.ds(start, rows), :]
        w_copies.append(pltpu.make_async_copy(piece, w.at[pl.ds(at, rows), :], w_sem.at[i]))
        at += rows
    for c in w_copies:
        c.start()

    for who, ref in enumerate((own_ref, peer_ref)):
        for g in range(groups):
            for h in range(heads):
                at = (g * heads + h) * HD
                for t in range(2):
                    row = (2 * who + t) * tokens
                    src = (2 * h + t) * HD
                    x[row : row + tokens, at : at + HD] = ref[g, :, src : src + HD]

    def part(weight_ref, begin):
        end = begin + weight_ref.shape[0]
        y = lax.dot_general(x[...], weight_ref[...], NT, preferred_element_type=F32)
        for who, ref in enumerate((mine_ref, send_ref)):
            lines = slice(first * PIECE + begin, first * PIECE + end)
            gate, gate_dot = (gates_ref[2 * who + t : 2 * who + t + 1, lines] for t in range(2))
            primal = y[2 * who * tokens : (2 * who + 1) * tokens]
            tangent = y[(2 * who + 1) * tokens : (2 * who + 2) * tokens]
            ref[0, :, begin:end] = (gate * primal).astype(BF16)
            ref[1, :, begin:end] = (gate_dot * primal + gate * tangent).astype(BF16)

    if ready_rows:
        part(ready, 0)
    for c in w_copies:
        c.wait()
    part(w, ready_rows)


def project(first, own, peer, gates, ready, weights, plan=None):
    groups, tokens, _ = own.shape
    n = len(weights)
    plan = plan or [(i, 0, a.shape[0]) for i, a in enumerate(weights)]
    rows = sum(count for _, _, count in plan)
    ready_rows = 0 if ready is None else ready.shape[0]
    depth = weights[0].shape[1]
    hbm = pl.BlockSpec(memory_space=pltpu.HBM)
    vmem = pl.BlockSpec(memory_space=pltpu.VMEM)
    half = jax.ShapeDtypeStruct((2, tokens, round_up(ready_rows + rows, HD)), BF16)
    return pl.pallas_call(
        functools.partial(project_body, n, first, ready_rows, plan),
        in_specs=[vmem] * (3 if ready is None else 4) + [hbm] * n,
        out_specs=[vmem, vmem],
        out_shape=[half, half],
        scratch_shapes=[
            pltpu.VMEM((4 * tokens, depth), BF16),
            pltpu.VMEM((rows, depth), BF16),
            pltpu.SemaphoreType.DMA((len(plan),)),
        ],
        compiler_params=pltpu.CompilerParams(vmem_limit_bytes=36 * MIB),
        cost_estimate=NO_COST,
        name="project",
    )(gates, own, peer, *(() if ready is None else (ready,)), *weights)


def merge_body(spots, info_ref, *refs):
    parts = (len(refs) - 2) // 2
    out_refs = refs[2 * parts :]
    first = info_ref[8] == 0
    for i, (part, at) in enumerate(spots):
        own_ref, got_ref = refs[part], refs[parts + part]
        cols = 2 * PIECE
        column = pl.multiple_of(info_ref[9 + i] * cols, cols)
        here = slice(at * PIECE, (at + 1) * PIECE)
        for t in range(2):
            own, got = own_ref[t, :, here], got_ref[t, :, here]
            low = jnp.where(first, own, got)
            high = jnp.where(first, got, own)
            out_refs[t][:, pl.ds(column, cols)] = jnp.concatenate([low, high], axis=1)


def merge(info, spots, owns, gots, width):
    tokens = owns[0].shape[1]
    vmem = pl.BlockSpec(memory_space=pltpu.VMEM)
    out = jax.ShapeDtypeStruct((tokens, width), BF16)
    return pl.pallas_call(
        functools.partial(merge_body, spots),
        in_specs=[pl.BlockSpec(memory_space=pltpu.SMEM)] + [vmem] * (2 * len(owns)),
        out_specs=[vmem, vmem],
        out_shape=[out, out],
        compiler_params=pltpu.CompilerParams(vmem_limit_bytes=12 * MIB),
        cost_estimate=NO_COST,
        name="merge",
    )(info, *owns, *gots)


def local(
    query_raw,
    key_raw,
    value_in,
    query_dot,
    key_dot,
    value_dot,
    gain_query,
    gain_key,
    out_weight,
    gate_table,
    gate_dot_table,
    time_index,
):
    groups = lax.axis_size("seq")
    fsdp = lax.axis_index("fsdp")
    core = fsdp % NC
    x_lo = fsdp // NC % NXL
    y = fsdp // (NC * NXL)
    up, down, swap = along_y(1), along_y(-1), core_swap()

    def exchange(a):
        return lax.all_to_all(a, "seq", split_axis=0, concat_axis=0, tiled=True)

    other = 1 - x_lo
    steps = (0, -1, 1, 2)
    block = [(y + step) % NY * NXL + low for low in (x_lo, other) for step in steps]
    source = [index * NC + core for index in block]
    info = jnp.stack([jnp.asarray(v, jnp.int32) for v in (*source, core, *block)])

    weight = out_weight.T
    half = PIECE // 2
    near = move(weight, beside())
    w1 = weight[:half]
    a1 = move(w1, up)
    b1 = move(w1, down)
    peer_time = move(time_index, swap)
    (packed,) = norm_pack(
        query_raw, query_dot, key_raw, key_dot, value_in, value_dot, gain_query, gain_key, groups, (3,)
    )
    times = jnp.concatenate([time_index, peer_time])
    packed, weight, near, a1, b1, times, info = lax.optimization_barrier(
        (packed, weight, near, a1, b1, times, info)
    )

    received = exchange(packed)
    w2 = weight[half:]
    a2 = move(w2, up)
    b2 = move(w2, down)
    c1 = move(a1, up)
    c2 = move(b2, down)
    quarter = half // 2
    near_a1 = move(near[:quarter], up)
    near_a2 = move(near[quarter:], up)
    near_b1 = move(near[quarter:half], down)
    near_b2 = move(jnp.concatenate([near[:quarter], near[half:]]), down)
    received, a2, b2, c1, c2 = lax.optimization_barrier((received, a2, b2, c1, c2))

    attn = attend(received, 0, 3)
    own = exchange(attn)
    gates, here = prepare(times, info, gate_table, gate_dot_table, (weight, a1, a2, b1, b2, c1, c2))
    own, near_a1, near_a2, near_b1, near_b2, gates, here, c2 = lax.optimization_barrier(
        (own, near_a1, near_a2, near_b1, near_b2, gates, here, c2)
    )

    peer = move(own, swap)
    near_c1 = move(near_a1, up)
    near_c2 = move(near_b1, down)
    near_c3 = move(c2, beside())

    mine_a, sent_a = project(
        0,
        own,
        peer,
        gates,
        here,
        (near, near_a1, near_a2, near_b1, near_b2),
        [(0, 0, PIECE), (1, 0, quarter), (2, 0, PIECE - quarter), (4, 0, quarter), (3, 0, quarter), (4, quarter, half)],
    )
    mine_a, sent_a, near_c1, near_c2, near_c3 = lax.optimization_barrier((mine_a, sent_a, near_c1, near_c2, near_c3))
    got_a = move(sent_a, swap)
    mine_b, sent_b = project(7, own, peer, gates, None, (near_c1, near_c2, near_c3))
    got_b = move(sent_b, swap)
    spots = [(0, i) for i in range(7)] + [(1, 0)]
    return tuple(merge(info, spots, (mine_a, mine_b), (got_a, got_b), gate_table.shape[1]))


def solution(mesh):
    return jax.shard_map(
        local,
        mesh=mesh,
        in_specs=(
            P(("fsdp", "seq"), None),
            P(("fsdp", "seq"), None),
            P(("fsdp", "seq"), None),
            P(("fsdp", "seq"), None),
            P(("fsdp", "seq"), None),
            P(("fsdp", "seq"), None),
            P(),
            P(),
            P(None, "fsdp"),
            P(),
            P(),
            P("fsdp"),
        ),
        out_specs=(P(("fsdp", "seq"), None), P(("fsdp", "seq"), None)),
        check_vma=False,
    )
```

```python
import functools
import math

import jax
import jax.numpy as jnp
from jax import lax
from jax.experimental import pallas as pl
from jax.experimental.pallas import tpu as pltpu
from jax.sharding import PartitionSpec as P

HD = 128
EPS = 1e-06
F32 = jnp.float32
BF16 = jnp.bfloat16
MIB = 1 << 20
VMEM_ALL = 60 * MIB
PIECE = 320
NO_COST = pl.CostEstimate(flops=0, bytes_accessed=0, transcendentals=0)

NY, NXL, NC, NXH, NZ = 4, 2, 2, 2, 4
NX = NXL * NXH


def place(y, x, core, z):
    x_hi, x_lo = divmod(x % NX, NXL)
    return (((y % NY) * NXL + x_lo) * NC + core) * (NXH * NZ) + x_hi * NZ + z


def chips():
    return [(y, x, z) for y in range(NY) for x in range(NX) for z in range(NZ)]


def along_y(step):
    return [(place(y, x, c, z), place(y + step, x, c, z)) for y, x, z in chips() for c in range(NC)]


def core_swap():
    return [(place(y, x, c, z), place(y, x, 1 - c, z)) for y, x, z in chips() for c in range(NC)]


def beside():
    return [(place(y, x, c, z), place(y, x + 1 - 2 * c, c, z)) for y, x, z in chips() for c in range(NC)]


def move(a, perm):
    return lax.ppermute(a, ("fsdp", "seq"), perm)


def norm_body(q_ref, qd_ref, k_ref, kd_ref, v_ref, vd_ref, gq_ref, gk_ref, *out_refs):
    def normed(raw_ref, dot_ref, gain_ref):
        signal = raw_ref[...].astype(F32)
        signal_dot = dot_ref[...].astype(F32)
        gain = gain_ref[...]
        inverse = lax.rsqrt(jnp.mean(signal * signal, axis=-1, keepdims=True) + EPS)
        inner = jnp.mean(signal * signal_dot, axis=-1, keepdims=True)
        hat = gain * signal * inverse
        hat_dot = gain * (signal_dot * inverse - signal * (inverse * inverse * inverse * inner))
        return hat.astype(BF16), hat_dot.astype(BF16)

    groups = out_refs[0].shape[0]
    counts = [ref.shape[2] // (6 * HD) for ref in out_refs]
    heads = sum(counts)
    target = [(ref, j) for ref, count in zip(out_refs, counts) for j in range(count)]
    q, qd = normed(q_ref, qd_ref, gq_ref)
    k, kd = normed(k_ref, kd_ref, gk_ref)
    pieces = (qd, q, k, kd, v_ref[...], vd_ref[...])
    for g in range(groups):
        for h in range(heads):
            src = (g * heads + h) * HD
            ref, j = target[h]
            for i, piece in enumerate(pieces):
                dst = (6 * j + i) * HD
                ref[g, :, dst : dst + HD] = piece[:, src : src + HD]


def norm_pack(q, qd, k, kd, v, vd, gq, gk, groups, counts):
    tokens, width = q.shape
    rows = 64
    wide = pl.BlockSpec((rows, width), lambda i: (i, 0))
    gain = pl.BlockSpec((1, width), lambda i: (0, 0))
    return pl.pallas_call(
        norm_body,
        grid=(tokens // rows,),
        in_specs=[wide] * 6 + [gain] * 2,
        out_specs=[pl.BlockSpec((groups, rows, n * 6 * HD), lambda i: (0, i, 0)) for n in counts],
        out_shape=[jax.ShapeDtypeStruct((groups, tokens, n * 6 * HD), BF16) for n in counts],
        compiler_params=pltpu.CompilerParams(vmem_limit_bytes=VMEM_ALL),
        cost_estimate=NO_COST,
        name="norm_pack",
    )(q, qd, k, kd, v, vd, gq.reshape(1, width), gk.reshape(1, width))


NT = (((1,), (1,)), ((), ()))
NN = (((1,), (0,)), ((), ()))


def attn_body(in_ref, *refs):
    out_ref = refs[-1]
    groups, tokens, _ = in_ref.shape
    length = groups * tokens
    blocks = 8
    rows = blocks * tokens
    scale = HD**-0.5

    def columns(first, count):
        return in_ref[:, :, first * HD : (first + count) * HD].reshape(length, count * HD)

    k, kk = columns(2, 1), columns(2, 2)
    v, vv = columns(4, 1), columns(4, 2)
    for b in range(0, groups, blocks):
        both = in_ref[b : b + blocks, :, 0 : 2 * HD].reshape(rows, 2 * HD)
        q = in_ref[b : b + blocks, :, HD : 2 * HD].reshape(rows, HD)
        s = lax.dot_general(q, k, NT, preferred_element_type=F32)
        sd = lax.dot_general(both, kk, NT, preferred_element_type=F32)
        peak = jnp.max(s, axis=-1, keepdims=True)
        w = jnp.exp2((s - peak) * (scale * math.log2(math.e)))
        inv = 1.0 / jnp.sum(w, axis=-1, keepdims=True)
        mean = jnp.sum(w * sd, axis=-1, keepdims=True) * inv
        w_dot = (w * (sd - mean)).astype(BF16)
        first = lax.dot_general(w.astype(BF16), vv, NN, preferred_element_type=F32)
        second = lax.dot_general(w_dot, v, NN, preferred_element_type=F32)
        attn = (first[:, :HD] * inv).astype(BF16)
        attn_dot = ((second * scale + first[:, HD:]) * inv).astype(BF16)
        out_ref[b : b + blocks, :, 0:HD] = attn.reshape(blocks, tokens, HD)
        out_ref[b : b + blocks, :, HD : 2 * HD] = attn_dot.reshape(blocks, tokens, HD)


def attend(packed, first, heads, earlier=None):
    groups, tokens, width = packed.shape
    return pl.pallas_call(
        attn_body,
        grid=(width // (6 * HD),),
        in_specs=[pl.BlockSpec((groups, tokens, 6 * HD), lambda h: (0, 0, h))]
        + ([] if earlier is None else [pl.BlockSpec(memory_space=pl.ANY)]),
        out_specs=pl.BlockSpec((groups, tokens, 2 * HD), lambda h: (0, 0, first + h)),
        out_shape=jax.ShapeDtypeStruct((groups, tokens, heads * 2 * HD), BF16),
        input_output_aliases={} if earlier is None else {1: 0},
        compiler_params=pltpu.CompilerParams(vmem_limit_bytes=VMEM_ALL),
        cost_estimate=NO_COST,
        name="attend",
    )(packed, *(() if earlier is None else (earlier,)))


def prepare_body(n, times_ref, info_ref, gate_hbm, gate_dot_hbm, *rest):
    weights = rest[:n]
    gates_ref, w_ref, wide, sem, w_sem = rest[n:]
    copies, at = [], 0
    for who in range(2):
        row = pl.multiple_of(times_ref[who] // 8 * 8, 8)
        for t, table in enumerate((gate_hbm, gate_dot_hbm)):
            copies.append(pltpu.make_async_copy(table.at[pl.ds(row, 8), :], wide.at[who, t], sem.at[who, t]))
    for i, weight in enumerate(weights):
        rows = weight.shape[0]
        copies.append(pltpu.make_async_copy(weight, w_ref.at[pl.ds(at, rows), :], w_sem.at[i]))
        at += rows
    for c in copies:
        c.start()
    for c in copies:
        c.wait()
    for who in range(2):
        row = times_ref[who] % 8
        for t in range(2):
            parts = []
            for i in range(gates_ref.shape[1] // PIECE):
                column = info_ref[i] * PIECE
                base = pl.multiple_of(column // HD * HD, HD)
                line = wide[who, t, pl.ds(row, 1), pl.ds(base, 3 * HD)]
                parts.append(jnp.where(column % HD != 0, line[:, HD // 2 : HD // 2 + PIECE], line[:, :PIECE]))
            gates_ref[2 * who + t : 2 * who + t + 1] = jnp.concatenate(parts, axis=1)


def prepare(times, info, gate_table, gate_dot_table, weights):
    width = gate_table.shape[1]
    n = len(weights)
    total = sum(a.shape[0] for a in weights)
    anywhere = pl.BlockSpec(memory_space=pl.ANY)
    depth = weights[0].shape[1]
    return pl.pallas_call(
        functools.partial(prepare_body, n),
        grid=(1,),
        in_specs=[pl.BlockSpec(memory_space=pltpu.SMEM)] * 2 + [anywhere] * (2 + n),
        out_specs=[pl.BlockSpec((8, 8 * PIECE), lambda i: (0, 0)), pl.BlockSpec((total, depth), lambda i: (0, 0))],
        out_shape=[
            jax.ShapeDtypeStruct((2048, 8 * PIECE), F32),
            jax.ShapeDtypeStruct((total, weights[0].shape[1]), BF16),
        ],
        scratch_shapes=[
            pltpu.VMEM((2, 2, 8, width), F32),
            pltpu.SemaphoreType.DMA((2, 2)),
            pltpu.SemaphoreType.DMA((n,)),
        ],
        compiler_params=pltpu.CompilerParams(vmem_limit_bytes=VMEM_ALL),
        cost_estimate=NO_COST,
        name="prepare",
    )(times, info, gate_table, gate_dot_table, *weights)


def round_up(n, unit):
    return -(-n // unit) * unit


def project_body(n, first, ready_rows, plan, gates_any, own_ref, peer_ref, *rest):
    ready = rest[0] if ready_rows else None
    rest = rest[1:] if ready_rows else rest
    weights = rest[:n]
    mine_ref, send_ref, x, w, gates_own, w_sem, g_sem = rest[n:]
    groups, tokens, _ = own_ref.shape
    heads = own_ref.shape[2] // (2 * HD)

    gates_ref = gates_any if ready_rows else gates_own
    at, w_copies = 0, []
    for i, (which, start, rows) in enumerate(plan):
        piece = weights[which].at[pl.ds(start, rows), :]
        w_copies.append(pltpu.make_async_copy(piece, w.at[pl.ds(at, rows), :], w_sem.at[i]))
        at += rows
    for c in w_copies:
        c.start()
    gates_copy = None
    if not ready_rows:
        gates_copy = pltpu.make_async_copy(gates_any.at[pl.ds(0, 8), :], gates_own, g_sem)
        gates_copy.start()

    for who, ref in enumerate((own_ref, peer_ref)):
        for g in range(groups):
            for h in range(heads):
                at = (g * heads + h) * HD
                for t in range(2):
                    row = (2 * who + t) * tokens
                    src = (2 * h + t) * HD
                    x[row : row + tokens, at : at + HD] = ref[g, :, src : src + HD]

    def part(weight_ref, begin):
        end = begin + weight_ref.shape[0]
        y = lax.dot_general(x[...], weight_ref[...], NT, preferred_element_type=F32)
        for who, ref in enumerate((mine_ref, send_ref)):
            lines = slice(first * PIECE + begin, first * PIECE + end)
            gate, gate_dot = (gates_ref[2 * who + t : 2 * who + t + 1, lines] for t in range(2))
            primal = y[2 * who * tokens : (2 * who + 1) * tokens]
            tangent = y[(2 * who + 1) * tokens : (2 * who + 2) * tokens]
            ref[0, :, begin:end] = (gate * primal).astype(BF16)
            ref[1, :, begin:end] = (gate_dot * primal + gate * tangent).astype(BF16)

    if ready_rows:
        part(ready, 0)
    else:
        gates_copy.wait()
    for c in w_copies:
        c.wait()
    part(w, ready_rows)


def whole(a):
    return pl.BlockSpec(a.shape, lambda i: (0,) * len(a.shape))


def project(first, own, peer, gates, ready, weights, plan=None):
    groups, tokens, _ = own.shape
    n = len(weights)
    plan = plan or [(i, 0, a.shape[0]) for i, a in enumerate(weights)]
    rows = sum(count for _, _, count in plan)
    ready_rows = 0 if ready is None else ready.shape[0]
    depth = weights[0].shape[1]
    hbm = pl.BlockSpec(memory_space=pltpu.HBM)
    half = jax.ShapeDtypeStruct((2, tokens, round_up(ready_rows + rows, HD)), BF16)
    return pl.pallas_call(
        functools.partial(project_body, n, first, ready_rows, plan),
        grid=(1,),
        in_specs=[hbm if ready is None else pl.BlockSpec((8, gates.shape[1]), lambda i: (0, 0))]
        + [whole(a) for a in ((own, peer) if ready is None else (own, peer, ready))]
        + [hbm] * n,
        out_specs=[whole(half), whole(half)],
        out_shape=[half, half],
        scratch_shapes=[
            pltpu.VMEM((4 * tokens, depth), BF16),
            pltpu.VMEM((rows, depth), BF16),
            pltpu.VMEM((8, gates.shape[1]), F32),
            pltpu.SemaphoreType.DMA((len(plan),)),
            pltpu.SemaphoreType.DMA,
        ],
        compiler_params=pltpu.CompilerParams(vmem_limit_bytes=36 * MIB),
        cost_estimate=NO_COST,
        name="project",
    )(gates, own, peer, *(() if ready is None else (ready,)), *weights)


def merge_body(spots, info_ref, *refs):
    parts = (len(refs) - 2) // 2
    out_refs = refs[2 * parts :]
    first = info_ref[8] == 0
    for i, (part, at) in enumerate(spots):
        own_ref, got_ref = refs[part], refs[parts + part]
        cols = 2 * PIECE
        column = pl.multiple_of(info_ref[9 + i] * cols, cols)
        here = slice(at * PIECE, (at + 1) * PIECE)
        for t in range(2):
            own, got = own_ref[t, :, here], got_ref[t, :, here]
            low = jnp.where(first, own, got)
            high = jnp.where(first, got, own)
            out_refs[t][:, pl.ds(column, cols)] = jnp.concatenate([low, high], axis=1)


def merge(info, spots, owns, gots, width):
    tokens = owns[0].shape[1]
    vmem = pl.BlockSpec(memory_space=pltpu.VMEM)
    out = jax.ShapeDtypeStruct((tokens, width), BF16)
    return pl.pallas_call(
        functools.partial(merge_body, spots),
        in_specs=[pl.BlockSpec(memory_space=pltpu.SMEM)] + [vmem] * (2 * len(owns)),
        out_specs=[vmem, vmem],
        out_shape=[out, out],
        compiler_params=pltpu.CompilerParams(vmem_limit_bytes=12 * MIB),
        cost_estimate=NO_COST,
        name="merge",
    )(info, *owns, *gots)


def local(
    query_raw,
    key_raw,
    value_in,
    query_dot,
    key_dot,
    value_dot,
    gain_query,
    gain_key,
    out_weight,
    gate_table,
    gate_dot_table,
    time_index,
):
    groups = lax.axis_size("seq")
    fsdp = lax.axis_index("fsdp")
    core = fsdp % NC
    x_lo = fsdp // NC % NXL
    y = fsdp // (NC * NXL)
    up, down, swap = along_y(1), along_y(-1), core_swap()

    def exchange(a):
        return lax.all_to_all(a, "seq", split_axis=0, concat_axis=0, tiled=True)

    other = 1 - x_lo
    steps = (0, -1, 1, 2)
    block = [(y + step) % NY * NXL + low for low in (x_lo, other) for step in steps]
    source = [index * NC + core for index in block]
    info = jnp.stack([jnp.asarray(v, jnp.int32) for v in (*source, core, *block)])

    weight = out_weight.T
    early = 160
    near = move(weight, beside())
    w1 = weight[:early]
    a1 = move(w1, up)
    b1 = move(w1, down)
    peer_time = move(time_index, swap)
    (packed,) = norm_pack(
        query_raw, query_dot, key_raw, key_dot, value_in, value_dot, gain_query, gain_key, groups, (3,)
    )
    times = jnp.concatenate([time_index, peer_time])
    packed, weight, near, a1, b1, times, info = lax.optimization_barrier(
        (packed, weight, near, a1, b1, times, info)
    )

    received = exchange(packed)
    w2 = weight[early:]
    a2 = move(w2, up)
    b2 = move(w2, down)
    c1 = move(a1, up)
    c2 = move(b2, down)
    quarter = PIECE // 4
    near_a1 = move(near[:quarter], up)
    near_a2 = move(near[quarter:], up)
    near_b1 = move(near[quarter:early], down)
    near_b2 = move(jnp.concatenate([near[:quarter], near[early:]]), down)
    received, a2, b2, c1, c2 = lax.optimization_barrier((received, a2, b2, c1, c2))

    attn = attend(received, 0, 3)
    own = exchange(attn)
    gates, here = prepare(times, info, gate_table, gate_dot_table, (weight, a1, a2, b1, b2, c1, c2))
    own, near_a1, near_a2, near_b1, near_b2, gates, here, c2 = lax.optimization_barrier(
        (own, near_a1, near_a2, near_b1, near_b2, gates, here, c2)
    )

    peer = move(own, swap)
    near_c1 = move(near_a1, up)
    near_c2 = move(near_b1, down)
    near_c3 = move(c2, beside())

    mine_a, sent_a = project(
        0,
        own,
        peer,
        gates,
        here,
        (near, near_a1, near_a2, near_b1, near_b2),
        [(0, 0, PIECE), (1, 0, quarter), (2, 0, PIECE - quarter), (4, 0, quarter), (3, 0, early - quarter), (4, quarter, PIECE - early)],
    )
    mine_a, sent_a, near_c1, near_c2, near_c3 = lax.optimization_barrier((mine_a, sent_a, near_c1, near_c2, near_c3))
    got_a = move(sent_a, swap)
    mine_b, sent_b = project(7, own, peer, gates, None, (near_c1, near_c2, near_c3))
    got_b = move(sent_b, swap)
    spots = [(0, i) for i in range(7)] + [(1, 0)]
    return tuple(merge(info, spots, (mine_a, mine_b), (got_a, got_b), gate_table.shape[1]))


def solution(mesh):
    return jax.shard_map(
        local,
        mesh=mesh,
        in_specs=(
            P(("fsdp", "seq"), None),
            P(("fsdp", "seq"), None),
            P(("fsdp", "seq"), None),
            P(("fsdp", "seq"), None),
            P(("fsdp", "seq"), None),
            P(("fsdp", "seq"), None),
            P(),
            P(),
            P(None, "fsdp"),
            P(),
            P(),
            P("fsdp"),
        ),
        out_specs=(P(("fsdp", "seq"), None), P(("fsdp", "seq"), None)),
        check_vma=False,
    )
```

```python
import functools
import math

import jax
import jax.numpy as jnp
from jax import lax
from jax.experimental import pallas as pl
from jax.experimental.pallas import tpu as pltpu
from jax.sharding import PartitionSpec as P

HD = 128
EPS = 1e-06
F32 = jnp.float32
BF16 = jnp.bfloat16
MIB = 1 << 20
VMEM_ALL = 60 * MIB
PIECE = 320
NO_COST = pl.CostEstimate(flops=0, bytes_accessed=0, transcendentals=0)

NY, NXL, NC, NXH, NZ = 4, 2, 2, 2, 4
NX = NXL * NXH


def place(y, x, core, z):
    x_hi, x_lo = divmod(x % NX, NXL)
    return (((y % NY) * NXL + x_lo) * NC + core) * (NXH * NZ) + x_hi * NZ + z


def chips():
    return [(y, x, z) for y in range(NY) for x in range(NX) for z in range(NZ)]


def along_y(step):
    return [(place(y, x, c, z), place(y + step, x, c, z)) for y, x, z in chips() for c in range(NC)]


def core_swap():
    return [(place(y, x, c, z), place(y, x, 1 - c, z)) for y, x, z in chips() for c in range(NC)]


def beside():
    return [(place(y, x, c, z), place(y, x + 1 - 2 * c, c, z)) for y, x, z in chips() for c in range(NC)]


def move(a, perm):
    return lax.ppermute(a, ("fsdp", "seq"), perm)


def norm_body(q_ref, qd_ref, k_ref, kd_ref, v_ref, vd_ref, gq_ref, gk_ref, *out_refs):
    def normed(raw_ref, dot_ref, gain_ref):
        signal = raw_ref[...].astype(F32)
        signal_dot = dot_ref[...].astype(F32)
        gain = gain_ref[...]
        inverse = lax.rsqrt(jnp.mean(signal * signal, axis=-1, keepdims=True) + EPS)
        inner = jnp.mean(signal * signal_dot, axis=-1, keepdims=True)
        hat = gain * signal * inverse
        hat_dot = gain * (signal_dot * inverse - signal * (inverse * inverse * inverse * inner))
        return hat.astype(BF16), hat_dot.astype(BF16)

    groups = out_refs[0].shape[0]
    counts = [ref.shape[2] // (6 * HD) for ref in out_refs]
    heads = sum(counts)
    target = [(ref, j) for ref, count in zip(out_refs, counts) for j in range(count)]
    q, qd = normed(q_ref, qd_ref, gq_ref)
    k, kd = normed(k_ref, kd_ref, gk_ref)
    pieces = (qd, q, k, kd, v_ref[...], vd_ref[...])
    for g in range(groups):
        for h in range(heads):
            src = (g * heads + h) * HD
            ref, j = target[h]
            for i, piece in enumerate(pieces):
                dst = (6 * j + i) * HD
                ref[g, :, dst : dst + HD] = piece[:, src : src + HD]


def norm_pack(q, qd, k, kd, v, vd, gq, gk, groups, counts):
    tokens, width = q.shape
    rows = 64
    wide = pl.BlockSpec((rows, width), lambda i: (i, 0))
    gain = pl.BlockSpec((1, width), lambda i: (0, 0))
    return pl.pallas_call(
        norm_body,
        grid=(tokens // rows,),
        in_specs=[wide] * 6 + [gain] * 2,
        out_specs=[pl.BlockSpec((groups, rows, n * 6 * HD), lambda i: (0, i, 0)) for n in counts],
        out_shape=[jax.ShapeDtypeStruct((groups, tokens, n * 6 * HD), BF16) for n in counts],
        compiler_params=pltpu.CompilerParams(vmem_limit_bytes=VMEM_ALL),
        cost_estimate=NO_COST,
        name="norm_pack",
    )(q, qd, k, kd, v, vd, gq.reshape(1, width), gk.reshape(1, width))


NT = (((1,), (1,)), ((), ()))
NN = (((1,), (0,)), ((), ()))


def attn_body(in_ref, *refs):
    out_ref = refs[-1]
    groups, tokens, _ = in_ref.shape
    length = groups * tokens
    blocks = 8
    rows = blocks * tokens
    scale = HD**-0.5

    def columns(first, count):
        return in_ref[:, :, first * HD : (first + count) * HD].reshape(length, count * HD)

    k, kk = columns(2, 1), columns(2, 2)
    v, vv = columns(4, 1), columns(4, 2)
    for b in range(0, groups, blocks):
        both = in_ref[b : b + blocks, :, 0 : 2 * HD].reshape(rows, 2 * HD)
        q = in_ref[b : b + blocks, :, HD : 2 * HD].reshape(rows, HD)
        s = lax.dot_general(q, k, NT, preferred_element_type=F32)
        sd = lax.dot_general(both, kk, NT, preferred_element_type=F32)
        peak = jnp.max(s, axis=-1, keepdims=True)
        w = jnp.exp2((s - peak) * (scale * math.log2(math.e)))
        inv = 1.0 / jnp.sum(w, axis=-1, keepdims=True)
        mean = jnp.sum(w * sd, axis=-1, keepdims=True) * inv
        w_dot = (w * (sd - mean)).astype(BF16)
        first = lax.dot_general(w.astype(BF16), vv, NN, preferred_element_type=F32)
        second = lax.dot_general(w_dot, v, NN, preferred_element_type=F32)
        attn = (first[:, :HD] * inv).astype(BF16)
        attn_dot = ((second * scale + first[:, HD:]) * inv).astype(BF16)
        out_ref[b : b + blocks, :, 0:HD] = attn.reshape(blocks, tokens, HD)
        out_ref[b : b + blocks, :, HD : 2 * HD] = attn_dot.reshape(blocks, tokens, HD)


def attend(packed, first, heads, earlier=None):
    groups, tokens, width = packed.shape
    return pl.pallas_call(
        attn_body,
        grid=(width // (6 * HD),),
        in_specs=[pl.BlockSpec((groups, tokens, 6 * HD), lambda h: (0, 0, h))]
        + ([] if earlier is None else [pl.BlockSpec(memory_space=pl.ANY)]),
        out_specs=pl.BlockSpec((groups, tokens, 2 * HD), lambda h: (0, 0, first + h)),
        out_shape=jax.ShapeDtypeStruct((groups, tokens, heads * 2 * HD), BF16),
        input_output_aliases={} if earlier is None else {1: 0},
        compiler_params=pltpu.CompilerParams(vmem_limit_bytes=VMEM_ALL),
        cost_estimate=NO_COST,
        name="attend",
    )(packed, *(() if earlier is None else (earlier,)))


def prepare_body(n, times_ref, info_ref, gate_hbm, gate_dot_hbm, *rest):
    weights = rest[:n]
    gates_ref, w_ref, wide, sem, w_sem = rest[n:]
    copies, at = [], 0
    for who in range(2):
        row = pl.multiple_of(times_ref[who] // 8 * 8, 8)
        for t, table in enumerate((gate_hbm, gate_dot_hbm)):
            copies.append(pltpu.make_async_copy(table.at[pl.ds(row, 8), :], wide.at[who, t], sem.at[who, t]))
    for i, weight in enumerate(weights):
        rows = weight.shape[0]
        copies.append(pltpu.make_async_copy(weight, w_ref.at[pl.ds(at, rows), :], w_sem.at[i]))
        at += rows
    for c in copies:
        c.start()
    for c in copies:
        c.wait()
    for who in range(2):
        row = times_ref[who] % 8
        for t in range(2):
            parts = []
            for i in range(gates_ref.shape[1] // PIECE):
                column = info_ref[i] * PIECE
                base = pl.multiple_of(column // HD * HD, HD)
                line = wide[who, t, pl.ds(row, 1), pl.ds(base, 3 * HD)]
                parts.append(jnp.where(column % HD != 0, line[:, HD // 2 : HD // 2 + PIECE], line[:, :PIECE]))
            gates_ref[2 * who + t : 2 * who + t + 1] = jnp.concatenate(parts, axis=1)


def prepare(times, info, gate_table, gate_dot_table, weights):
    width = gate_table.shape[1]
    n = len(weights)
    total = sum(a.shape[0] for a in weights)
    anywhere = pl.BlockSpec(memory_space=pl.ANY)
    depth = weights[0].shape[1]
    return pl.pallas_call(
        functools.partial(prepare_body, n),
        grid=(1,),
        in_specs=[pl.BlockSpec(memory_space=pltpu.SMEM)] * 2 + [anywhere] * (2 + n),
        out_specs=[pl.BlockSpec((8, 8 * PIECE), lambda i: (0, 0)), pl.BlockSpec((total, depth), lambda i: (0, 0))],
        out_shape=[
            jax.ShapeDtypeStruct((2048, 8 * PIECE), F32),
            jax.ShapeDtypeStruct((total, weights[0].shape[1]), BF16),
        ],
        scratch_shapes=[
            pltpu.VMEM((2, 2, 8, width), F32),
            pltpu.SemaphoreType.DMA((2, 2)),
            pltpu.SemaphoreType.DMA((n,)),
        ],
        compiler_params=pltpu.CompilerParams(vmem_limit_bytes=VMEM_ALL),
        cost_estimate=NO_COST,
        name="prepare",
    )(times, info, gate_table, gate_dot_table, *weights)


def round_up(n, unit):
    return -(-n // unit) * unit


def project_body(n, first, ready_rows, plan, gates_any, own_ref, peer_ref, *rest):
    ready = rest[0] if ready_rows else None
    rest = rest[1:] if ready_rows else rest
    weights = rest[:n]
    mine_ref, send_ref, x, w, gates_own, w_sem, g_sem = rest[n:]
    groups, tokens, _ = own_ref.shape
    heads = own_ref.shape[2] // (2 * HD)

    gates_ref = gates_any if ready_rows else gates_own
    at, w_copies = 0, []
    for i, (which, start, rows) in enumerate(plan):
        piece = weights[which].at[pl.ds(start, rows), :]
        w_copies.append(pltpu.make_async_copy(piece, w.at[pl.ds(at, rows), :], w_sem.at[i]))
        at += rows
    for c in w_copies:
        c.start()
    gates_copy = None
    if not ready_rows:
        gates_copy = pltpu.make_async_copy(gates_any.at[pl.ds(0, 8), :], gates_own, g_sem)
        gates_copy.start()

    for who, ref in enumerate((own_ref, peer_ref)):
        for g in range(groups):
            for h in range(heads):
                at = (g * heads + h) * HD
                for t in range(2):
                    row = (2 * who + t) * tokens
                    src = (2 * h + t) * HD
                    x[row : row + tokens, at : at + HD] = ref[g, :, src : src + HD]

    def part(weight_ref, begin):
        end = begin + weight_ref.shape[0]
        y = lax.dot_general(x[...], weight_ref[...], NT, preferred_element_type=F32)
        for who, ref in enumerate((mine_ref, send_ref)):
            lines = slice(first * PIECE + begin, first * PIECE + end)
            gate, gate_dot = (gates_ref[2 * who + t : 2 * who + t + 1, lines] for t in range(2))
            primal = y[2 * who * tokens : (2 * who + 1) * tokens]
            tangent = y[(2 * who + 1) * tokens : (2 * who + 2) * tokens]
            ref[0, :, begin:end] = (gate * primal).astype(BF16)
            ref[1, :, begin:end] = (gate_dot * primal + gate * tangent).astype(BF16)

    if ready_rows:
        part(ready, 0)
    else:
        gates_copy.wait()
    for c in w_copies:
        c.wait()
    part(w, ready_rows)


def whole(a):
    return pl.BlockSpec(a.shape, lambda i: (0,) * len(a.shape))


def project(first, own, peer, gates, ready, weights, plan=None):
    groups, tokens, _ = own.shape
    n = len(weights)
    plan = plan or [(i, 0, a.shape[0]) for i, a in enumerate(weights)]
    rows = sum(count for _, _, count in plan)
    ready_rows = 0 if ready is None else ready.shape[0]
    depth = weights[0].shape[1]
    hbm = pl.BlockSpec(memory_space=pltpu.HBM)
    half = jax.ShapeDtypeStruct((2, tokens, round_up(ready_rows + rows, HD)), BF16)
    return pl.pallas_call(
        functools.partial(project_body, n, first, ready_rows, plan),
        grid=(1,),
        in_specs=[hbm if ready is None else pl.BlockSpec((8, gates.shape[1]), lambda i: (0, 0))]
        + [whole(a) for a in ((own, peer) if ready is None else (own, peer, ready))]
        + [hbm] * n,
        out_specs=[whole(half), whole(half)],
        out_shape=[half, half],
        scratch_shapes=[
            pltpu.VMEM((4 * tokens, depth), BF16),
            pltpu.VMEM((rows, depth), BF16),
            pltpu.VMEM((8, gates.shape[1]), F32),
            pltpu.SemaphoreType.DMA((len(plan),)),
            pltpu.SemaphoreType.DMA,
        ],
        compiler_params=pltpu.CompilerParams(vmem_limit_bytes=36 * MIB),
        cost_estimate=NO_COST,
        name="project",
    )(gates, own, peer, *(() if ready is None else (ready,)), *weights)


def merge_body(spots, info_ref, *refs):
    parts = (len(refs) - 2) // 2
    out_refs = refs[2 * parts :]
    first = info_ref[8] == 0
    for i, (part, at) in enumerate(spots):
        own_ref, got_ref = refs[part], refs[parts + part]
        cols = 2 * PIECE
        column = pl.multiple_of(info_ref[9 + i] * cols, cols)
        here = slice(at * PIECE, (at + 1) * PIECE)
        for t in range(2):
            own, got = own_ref[t, :, here], got_ref[t, :, here]
            low = jnp.where(first, own, got)
            high = jnp.where(first, got, own)
            out_refs[t][:, pl.ds(column, cols)] = jnp.concatenate([low, high], axis=1)


def merge(info, spots, owns, gots, width):
    tokens = owns[0].shape[1]
    vmem = pl.BlockSpec(memory_space=pltpu.VMEM)
    out = jax.ShapeDtypeStruct((tokens, width), BF16)
    return pl.pallas_call(
        functools.partial(merge_body, spots),
        in_specs=[pl.BlockSpec(memory_space=pltpu.SMEM)] + [vmem] * (2 * len(owns)),
        out_specs=[vmem, vmem],
        out_shape=[out, out],
        compiler_params=pltpu.CompilerParams(vmem_limit_bytes=12 * MIB),
        cost_estimate=NO_COST,
        name="merge",
    )(info, *owns, *gots)


def local(
    query_raw,
    key_raw,
    value_in,
    query_dot,
    key_dot,
    value_dot,
    gain_query,
    gain_key,
    out_weight,
    gate_table,
    gate_dot_table,
    time_index,
):
    groups = lax.axis_size("seq")
    fsdp = lax.axis_index("fsdp")
    core = fsdp % NC
    x_lo = fsdp // NC % NXL
    y = fsdp // (NC * NXL)
    up, down, swap = along_y(1), along_y(-1), core_swap()

    def exchange(a):
        return lax.all_to_all(a, "seq", split_axis=0, concat_axis=0, tiled=True)

    other = 1 - x_lo
    steps = (0, -1, 1, 2)
    block = [(y + step) % NY * NXL + low for low in (x_lo, other) for step in steps]
    source = [index * NC + core for index in block]
    info = jnp.stack([jnp.asarray(v, jnp.int32) for v in (*source, core, *block)])

    weight = out_weight.T
    early = 160
    near = move(weight, beside())
    w1 = weight[:early]
    a1 = move(w1, up)
    b1 = move(w1, down)
    peer_time = move(time_index, swap)
    (packed,) = norm_pack(
        query_raw, query_dot, key_raw, key_dot, value_in, value_dot, gain_query, gain_key, groups, (3,)
    )
    times = jnp.concatenate([time_index, peer_time])
    packed, weight, near, a1, b1, times, info = lax.optimization_barrier(
        (packed, weight, near, a1, b1, times, info)
    )

    received = exchange(packed)
    w2 = weight[early:]
    a2 = move(w2, up)
    b2 = move(w2, down)
    c1 = move(a1, up)
    c2 = move(b2, down)
    quarter = PIECE // 4
    near_a1 = move(near[:quarter], up)
    near_a2 = move(near[quarter:], up)
    near_b1 = move(near[quarter:early], down)
    near_b2 = move(jnp.concatenate([near[:quarter], near[early:]]), down)
    received, a2, b2, c1, c2 = lax.optimization_barrier((received, a2, b2, c1, c2))

    attn = attend(received, 0, 3)
    own = exchange(attn)
    gates, here = prepare(times, info, gate_table, gate_dot_table, (weight, a1, a2, b1, b2, c1, c2))
    own, near_a2, near_b2, gates, here, c2 = lax.optimization_barrier((own, near_a2, near_b2, gates, here, c2))
    own, near_a1, near_b1 = lax.optimization_barrier((own, near_a1, near_b1))

    peer = move(own, swap)
    near_c1 = move(near_a1, up)
    near_c2 = move(near_b1, down)
    near_c3 = move(c2, beside())

    mine_a, sent_a = project(
        0,
        own,
        peer,
        gates,
        here,
        (near, near_a1, near_a2, near_b1, near_b2),
        [(0, 0, PIECE), (1, 0, quarter), (2, 0, PIECE - quarter), (4, 0, quarter), (3, 0, early - quarter), (4, quarter, PIECE - early)],
    )
    mine_a, sent_a, near_c1, near_c2, near_c3 = lax.optimization_barrier((mine_a, sent_a, near_c1, near_c2, near_c3))
    got_a = move(sent_a, swap)
    mine_b, sent_b = project(7, own, peer, gates, None, (near_c1, near_c2, near_c3))
    got_b = move(sent_b, swap)
    spots = [(0, i) for i in range(7)] + [(1, 0)]
    return tuple(merge(info, spots, (mine_a, mine_b), (got_a, got_b), gate_table.shape[1]))


def solution(mesh):
    return jax.shard_map(
        local,
        mesh=mesh,
        in_specs=(
            P(("fsdp", "seq"), None),
            P(("fsdp", "seq"), None),
            P(("fsdp", "seq"), None),
            P(("fsdp", "seq"), None),
            P(("fsdp", "seq"), None),
            P(("fsdp", "seq"), None),
            P(),
            P(),
            P(None, "fsdp"),
            P(),
            P(),
            P("fsdp"),
        ),
        out_specs=(P(("fsdp", "seq"), None), P(("fsdp", "seq"), None)),
        check_vma=False,
    )
```

```python
import functools
import math

import jax
import jax.numpy as jnp
from jax import lax
from jax.experimental import pallas as pl
from jax.experimental.pallas import tpu as pltpu
from jax.sharding import PartitionSpec as P

HD = 128
EPS = 1e-06
F32 = jnp.float32
BF16 = jnp.bfloat16
MIB = 1 << 20
VMEM_ALL = 60 * MIB
PIECE = 320
NO_COST = pl.CostEstimate(flops=0, bytes_accessed=0, transcendentals=0)

NY, NXL, NC, NXH, NZ = 4, 2, 2, 2, 4
NX = NXL * NXH


def place(y, x, core, z):
    x_hi, x_lo = divmod(x % NX, NXL)
    return (((y % NY) * NXL + x_lo) * NC + core) * (NXH * NZ) + x_hi * NZ + z


def chips():
    return [(y, x, z) for y in range(NY) for x in range(NX) for z in range(NZ)]


def along_y(step):
    return [(place(y, x, c, z), place(y + step, x, c, z)) for y, x, z in chips() for c in range(NC)]


def core_swap():
    return [(place(y, x, c, z), place(y, x, 1 - c, z)) for y, x, z in chips() for c in range(NC)]


def beside():
    return [(place(y, x, c, z), place(y, x + 1 - 2 * c, c, z)) for y, x, z in chips() for c in range(NC)]


def move(a, perm):
    return lax.ppermute(a, ("fsdp", "seq"), perm)


def norm_body(q_ref, qd_ref, k_ref, kd_ref, v_ref, vd_ref, gq_ref, gk_ref, *out_refs):
    def normed(raw_ref, dot_ref, gain_ref):
        signal = raw_ref[...].astype(F32)
        signal_dot = dot_ref[...].astype(F32)
        gain = gain_ref[...]
        inverse = lax.rsqrt(jnp.mean(signal * signal, axis=-1, keepdims=True) + EPS)
        inner = jnp.mean(signal * signal_dot, axis=-1, keepdims=True)
        hat = gain * signal * inverse
        hat_dot = gain * (signal_dot * inverse - signal * (inverse * inverse * inverse * inner))
        return hat.astype(BF16), hat_dot.astype(BF16)

    groups = out_refs[0].shape[0]
    counts = [ref.shape[2] // (6 * HD) for ref in out_refs]
    heads = sum(counts)
    target = [(ref, j) for ref, count in zip(out_refs, counts) for j in range(count)]
    q, qd = normed(q_ref, qd_ref, gq_ref)
    k, kd = normed(k_ref, kd_ref, gk_ref)
    pieces = (qd, q, k, kd, v_ref[...], vd_ref[...])
    for g in range(groups):
        for h in range(heads):
            src = (g * heads + h) * HD
            ref, j = target[h]
            for i, piece in enumerate(pieces):
                dst = (6 * j + i) * HD
                ref[g, :, dst : dst + HD] = piece[:, src : src + HD]


def norm_pack(q, qd, k, kd, v, vd, gq, gk, groups, counts):
    tokens, width = q.shape
    rows = 64
    wide = pl.BlockSpec((rows, width), lambda i: (i, 0))
    gain = pl.BlockSpec((1, width), lambda i: (0, 0))
    return pl.pallas_call(
        norm_body,
        grid=(tokens // rows,),
        in_specs=[wide] * 6 + [gain] * 2,
        out_specs=[pl.BlockSpec((groups, rows, n * 6 * HD), lambda i: (0, i, 0)) for n in counts],
        out_shape=[jax.ShapeDtypeStruct((groups, tokens, n * 6 * HD), BF16) for n in counts],
        compiler_params=pltpu.CompilerParams(vmem_limit_bytes=VMEM_ALL),
        cost_estimate=NO_COST,
        name="norm_pack",
    )(q, qd, k, kd, v, vd, gq.reshape(1, width), gk.reshape(1, width))


NT = (((1,), (1,)), ((), ()))
NN = (((1,), (0,)), ((), ()))


def attn_body(in_ref, *refs):
    out_ref = refs[-1]
    groups, tokens, _ = in_ref.shape
    length = groups * tokens
    blocks = 8
    rows = blocks * tokens
    scale = HD**-0.5

    def columns(first, count):
        return in_ref[:, :, first * HD : (first + count) * HD].reshape(length, count * HD)

    k, kk = columns(2, 1), columns(2, 2)
    v, vv = columns(4, 1), columns(4, 2)
    for b in range(0, groups, blocks):
        both = in_ref[b : b + blocks, :, 0 : 2 * HD].reshape(rows, 2 * HD)
        q = in_ref[b : b + blocks, :, HD : 2 * HD].reshape(rows, HD)
        s = lax.dot_general(q, k, NT, preferred_element_type=F32)
        sd = lax.dot_general(both, kk, NT, preferred_element_type=F32)
        peak = jnp.max(s, axis=-1, keepdims=True)
        w = jnp.exp2((s - peak) * (scale * math.log2(math.e)))
        inv = 1.0 / jnp.sum(w, axis=-1, keepdims=True)
        mean = jnp.sum(w * sd, axis=-1, keepdims=True) * inv
        w_dot = (w * (sd - mean)).astype(BF16)
        first = lax.dot_general(w.astype(BF16), vv, NN, preferred_element_type=F32)
        second = lax.dot_general(w_dot, v, NN, preferred_element_type=F32)
        attn = (first[:, :HD] * inv).astype(BF16)
        attn_dot = ((second * scale + first[:, HD:]) * inv).astype(BF16)
        out_ref[b : b + blocks, :, 0:HD] = attn.reshape(blocks, tokens, HD)
        out_ref[b : b + blocks, :, HD : 2 * HD] = attn_dot.reshape(blocks, tokens, HD)


def attend(packed, first, heads, earlier=None):
    groups, tokens, width = packed.shape
    return pl.pallas_call(
        attn_body,
        grid=(width // (6 * HD),),
        in_specs=[pl.BlockSpec((groups, tokens, 6 * HD), lambda h: (0, 0, h))]
        + ([] if earlier is None else [pl.BlockSpec(memory_space=pl.ANY)]),
        out_specs=pl.BlockSpec((groups, tokens, 2 * HD), lambda h: (0, 0, first + h)),
        out_shape=jax.ShapeDtypeStruct((groups, tokens, heads * 2 * HD), BF16),
        input_output_aliases={} if earlier is None else {1: 0},
        compiler_params=pltpu.CompilerParams(vmem_limit_bytes=VMEM_ALL),
        cost_estimate=NO_COST,
        name="attend",
    )(packed, *(() if earlier is None else (earlier,)))


def prepare_body(n, times_ref, info_ref, gate_hbm, gate_dot_hbm, *rest):
    weights = rest[:n]
    gates_ref, w_ref, wide, sem, w_sem = rest[n:]
    copies, at = [], 0
    for who in range(2):
        row = pl.multiple_of(times_ref[who] // 8 * 8, 8)
        for t, table in enumerate((gate_hbm, gate_dot_hbm)):
            copies.append(pltpu.make_async_copy(table.at[pl.ds(row, 8), :], wide.at[who, t], sem.at[who, t]))
    for i, weight in enumerate(weights):
        rows = weight.shape[0]
        copies.append(pltpu.make_async_copy(weight, w_ref.at[pl.ds(at, rows), :], w_sem.at[i]))
        at += rows
    for c in copies:
        c.start()
    for c in copies:
        c.wait()
    for who in range(2):
        row = times_ref[who] % 8
        for t in range(2):
            parts = []
            for i in range(gates_ref.shape[1] // PIECE):
                column = info_ref[i] * PIECE
                base = pl.multiple_of(column // HD * HD, HD)
                line = wide[who, t, pl.ds(row, 1), pl.ds(base, 3 * HD)]
                parts.append(jnp.where(column % HD != 0, line[:, HD // 2 : HD // 2 + PIECE], line[:, :PIECE]))
            gates_ref[2 * who + t : 2 * who + t + 1] = jnp.concatenate(parts, axis=1)


def prepare(times, info, gate_table, gate_dot_table, weights):
    width = gate_table.shape[1]
    n = len(weights)
    total = sum(a.shape[0] for a in weights)
    anywhere = pl.BlockSpec(memory_space=pl.ANY)
    depth = weights[0].shape[1]
    return pl.pallas_call(
        functools.partial(prepare_body, n),
        grid=(1,),
        in_specs=[pl.BlockSpec(memory_space=pltpu.SMEM)] * 2 + [anywhere] * (2 + n),
        out_specs=[pl.BlockSpec((8, 8 * PIECE), lambda i: (0, 0)), pl.BlockSpec((total, depth), lambda i: (0, 0))],
        out_shape=[
            jax.ShapeDtypeStruct((2048, 8 * PIECE), F32),
            jax.ShapeDtypeStruct((total, weights[0].shape[1]), BF16),
        ],
        scratch_shapes=[
            pltpu.VMEM((2, 2, 8, width), F32),
            pltpu.SemaphoreType.DMA((2, 2)),
            pltpu.SemaphoreType.DMA((n,)),
        ],
        compiler_params=pltpu.CompilerParams(vmem_limit_bytes=VMEM_ALL),
        cost_estimate=NO_COST,
        name="prepare",
    )(times, info, gate_table, gate_dot_table, *weights)


def round_up(n, unit):
    return -(-n // unit) * unit


def project_body(n, first, ready_rows, plan, gates_any, own_ref, peer_ref, *rest):
    ready = rest[0] if ready_rows else None
    rest = rest[1:] if ready_rows else rest
    weights = rest[:n]
    mine_ref, send_ref, x, w, gates_own, w_sem, g_sem = rest[n:]
    groups, tokens, _ = own_ref.shape
    heads = own_ref.shape[2] // (2 * HD)

    gates_ref = gates_any if ready_rows else gates_own
    at, w_copies = 0, []
    for i, (which, start, rows) in enumerate(plan):
        piece = weights[which].at[pl.ds(start, rows), :]
        w_copies.append(pltpu.make_async_copy(piece, w.at[pl.ds(at, rows), :], w_sem.at[i]))
        at += rows
    for c in w_copies:
        c.start()
    gates_copy = None
    if not ready_rows:
        gates_copy = pltpu.make_async_copy(gates_any.at[pl.ds(0, 8), :], gates_own, g_sem)
        gates_copy.start()

    for who, ref in enumerate((own_ref, peer_ref)):
        for g in range(groups):
            for h in range(heads):
                at = (g * heads + h) * HD
                for t in range(2):
                    row = (2 * who + t) * tokens
                    src = (2 * h + t) * HD
                    x[row : row + tokens, at : at + HD] = ref[g, :, src : src + HD]

    def part(weight_ref, begin):
        end = begin + weight_ref.shape[0]
        y = lax.dot_general(x[...], weight_ref[...], NT, preferred_element_type=F32)
        for who, ref in enumerate((mine_ref, send_ref)):
            lines = slice(first * PIECE + begin, first * PIECE + end)
            gate, gate_dot = (gates_ref[2 * who + t : 2 * who + t + 1, lines] for t in range(2))
            primal = y[2 * who * tokens : (2 * who + 1) * tokens]
            tangent = y[(2 * who + 1) * tokens : (2 * who + 2) * tokens]
            ref[0, :, begin:end] = (gate * primal).astype(BF16)
            ref[1, :, begin:end] = (gate_dot * primal + gate * tangent).astype(BF16)

    if ready_rows:
        part(ready, 0)
    else:
        gates_copy.wait()
    for c in w_copies:
        c.wait()
    part(w, ready_rows)


def whole(a):
    return pl.BlockSpec(a.shape, lambda i: (0,) * len(a.shape))


def project(first, own, peer, gates, ready, weights, plan=None):
    groups, tokens, _ = own.shape
    n = len(weights)
    plan = plan or [(i, 0, a.shape[0]) for i, a in enumerate(weights)]
    rows = sum(count for _, _, count in plan)
    ready_rows = 0 if ready is None else ready.shape[0]
    depth = weights[0].shape[1]
    hbm = pl.BlockSpec(memory_space=pltpu.HBM)
    half = jax.ShapeDtypeStruct((2, tokens, round_up(ready_rows + rows, HD)), BF16)
    return pl.pallas_call(
        functools.partial(project_body, n, first, ready_rows, plan),
        grid=(1,),
        in_specs=[hbm if ready is None else pl.BlockSpec((8, gates.shape[1]), lambda i: (0, 0))]
        + [whole(a) for a in ((own, peer) if ready is None else (own, peer, ready))]
        + [hbm] * n,
        out_specs=[whole(half), whole(half)],
        out_shape=[half, half],
        scratch_shapes=[
            pltpu.VMEM((4 * tokens, depth), BF16),
            pltpu.VMEM((rows, depth), BF16),
            pltpu.VMEM((8, gates.shape[1]), F32),
            pltpu.SemaphoreType.DMA((len(plan),)),
            pltpu.SemaphoreType.DMA,
        ],
        compiler_params=pltpu.CompilerParams(vmem_limit_bytes=36 * MIB),
        cost_estimate=NO_COST,
        name="project",
    )(gates, own, peer, *(() if ready is None else (ready,)), *weights)


def merge_body(spots, info_ref, *refs):
    parts = (len(refs) - 4) // 2
    out_hbm = refs[2 * parts : 2 * parts + 2]
    outs, sem = refs[2 * parts + 2 :]
    first = info_ref[8] == 0
    copies = []
    for t in range(2):
        for i, (part, at) in enumerate(spots):
            own_ref, got_ref = refs[part], refs[parts + part]
            cols = 2 * PIECE
            column = pl.multiple_of(info_ref[9 + i] * cols, cols)
            here = slice(at * PIECE, (at + 1) * PIECE)
            own, got = own_ref[t, :, here], got_ref[t, :, here]
            low = jnp.where(first, own, got)
            high = jnp.where(first, got, own)
            outs[t, :, pl.ds(column, cols)] = jnp.concatenate([low, high], axis=1)
        copies.append(pltpu.make_async_copy(outs.at[t], out_hbm[t], sem.at[t]))
        copies[t].start()
    for c in copies:
        c.wait()


def merge(info, spots, owns, gots, width):
    tokens = owns[0].shape[1]
    vmem = pl.BlockSpec(memory_space=pltpu.VMEM)
    anywhere = pl.BlockSpec(memory_space=pl.ANY)
    out = jax.ShapeDtypeStruct((tokens, width), BF16)
    return pl.pallas_call(
        functools.partial(merge_body, spots),
        in_specs=[pl.BlockSpec(memory_space=pltpu.SMEM)] + [vmem] * (2 * len(owns)),
        out_specs=[anywhere, anywhere],
        out_shape=[out, out],
        scratch_shapes=[pltpu.VMEM((2, tokens, width), BF16), pltpu.SemaphoreType.DMA((2,))],
        compiler_params=pltpu.CompilerParams(vmem_limit_bytes=12 * MIB),
        cost_estimate=NO_COST,
        name="merge",
    )(info, *owns, *gots)


def local(
    query_raw,
    key_raw,
    value_in,
    query_dot,
    key_dot,
    value_dot,
    gain_query,
    gain_key,
    out_weight,
    gate_table,
    gate_dot_table,
    time_index,
):
    groups = lax.axis_size("seq")
    fsdp = lax.axis_index("fsdp")
    core = fsdp % NC
    x_lo = fsdp // NC % NXL
    y = fsdp // (NC * NXL)
    up, down, swap = along_y(1), along_y(-1), core_swap()

    def exchange(a):
        return lax.all_to_all(a, "seq", split_axis=0, concat_axis=0, tiled=True)

    other = 1 - x_lo
    steps = (0, -1, 1, 2)
    block = [(y + step) % NY * NXL + low for low in (x_lo, other) for step in steps]
    source = [index * NC + core for index in block]
    info = jnp.stack([jnp.asarray(v, jnp.int32) for v in (*source, core, *block)])

    weight = out_weight.T
    early = 160
    near = move(weight, beside())
    w1 = weight[:early]
    a1 = move(w1, up)
    b1 = move(w1, down)
    peer_time = move(time_index, swap)
    (packed,) = norm_pack(
        query_raw, query_dot, key_raw, key_dot, value_in, value_dot, gain_query, gain_key, groups, (3,)
    )
    times = jnp.concatenate([time_index, peer_time])
    packed, weight, near, a1, b1, times, info = lax.optimization_barrier(
        (packed, weight, near, a1, b1, times, info)
    )

    received = exchange(packed)
    w2 = weight[early:]
    a2 = move(w2, up)
    b2 = move(w2, down)
    c1 = move(a1, up)
    c2 = move(b2, down)
    quarter = PIECE // 4
    near_a1 = move(near[:quarter], up)
    near_a2 = move(near[quarter:], up)
    near_b1 = move(near[quarter:early], down)
    near_b2 = move(jnp.concatenate([near[:quarter], near[early:]]), down)
    received, a2, b2, c1, c2 = lax.optimization_barrier((received, a2, b2, c1, c2))

    attn = attend(received, 0, 3)
    own = exchange(attn)
    gates, here = prepare(times, info, gate_table, gate_dot_table, (weight, a1, a2, b1, b2, c1, c2))
    own, near_a2, near_b2, gates, here, c2 = lax.optimization_barrier((own, near_a2, near_b2, gates, here, c2))
    own, near_a1, near_b1 = lax.optimization_barrier((own, near_a1, near_b1))

    peer = move(own, swap)
    near_c1 = move(near_a1, up)
    near_c2 = move(near_b1, down)
    near_c3 = move(c2, beside())

    mine_a, sent_a = project(
        0,
        own,
        peer,
        gates,
        here,
        (near, near_a1, near_a2, near_b1, near_b2),
        [(0, 0, PIECE), (1, 0, quarter), (2, 0, PIECE - quarter), (4, 0, quarter), (3, 0, early - quarter), (4, quarter, PIECE - early)],
    )
    mine_a, sent_a, near_c1, near_c2, near_c3 = lax.optimization_barrier((mine_a, sent_a, near_c1, near_c2, near_c3))
    got_a = move(sent_a, swap)
    mine_b, sent_b = project(7, own, peer, gates, None, (near_c1, near_c2, near_c3))
    got_b = move(sent_b, swap)
    spots = [(0, i) for i in range(7)] + [(1, 0)]
    return tuple(merge(info, spots, (mine_a, mine_b), (got_a, got_b), gate_table.shape[1]))


def solution(mesh):
    return jax.shard_map(
        local,
        mesh=mesh,
        in_specs=(
            P(("fsdp", "seq"), None),
            P(("fsdp", "seq"), None),
            P(("fsdp", "seq"), None),
            P(("fsdp", "seq"), None),
            P(("fsdp", "seq"), None),
            P(("fsdp", "seq"), None),
            P(),
            P(),
            P(None, "fsdp"),
            P(),
            P(),
            P("fsdp"),
        ),
        out_specs=(P(("fsdp", "seq"), None), P(("fsdp", "seq"), None)),
        check_vma=False,
    )
```

```python
import functools
import math

import jax
import jax.numpy as jnp
from jax import lax
from jax.experimental import pallas as pl
from jax.experimental.pallas import tpu as pltpu
from jax.sharding import PartitionSpec as P

HD = 128
EPS = 1e-06
F32 = jnp.float32
BF16 = jnp.bfloat16
MIB = 1 << 20
VMEM_ALL = 60 * MIB
PIECE = 320
NO_COST = pl.CostEstimate(flops=0, bytes_accessed=0, transcendentals=0)

NY, NXL, NC, NXH, NZ = 4, 2, 2, 2, 4
NX = NXL * NXH


def place(y, x, core, z):
    x_hi, x_lo = divmod(x % NX, NXL)
    return (((y % NY) * NXL + x_lo) * NC + core) * (NXH * NZ) + x_hi * NZ + z


def chips():
    return [(y, x, z) for y in range(NY) for x in range(NX) for z in range(NZ)]


def along_y(step):
    return [(place(y, x, c, z), place(y + step, x, c, z)) for y, x, z in chips() for c in range(NC)]


def core_swap():
    return [(place(y, x, c, z), place(y, x, 1 - c, z)) for y, x, z in chips() for c in range(NC)]


def beside():
    return [(place(y, x, c, z), place(y, x + 1 - 2 * c, c, z)) for y, x, z in chips() for c in range(NC)]


def move(a, perm):
    return lax.ppermute(a, ("fsdp", "seq"), perm)


def norm_body(q_ref, qd_ref, k_ref, kd_ref, v_ref, vd_ref, gq_ref, gk_ref, *out_refs):
    def normed(raw_ref, dot_ref, gain_ref):
        signal = raw_ref[...].astype(F32)
        signal_dot = dot_ref[...].astype(F32)
        gain = gain_ref[...]
        inverse = lax.rsqrt(jnp.mean(signal * signal, axis=-1, keepdims=True) + EPS)
        inner = jnp.mean(signal * signal_dot, axis=-1, keepdims=True)
        hat = gain * signal * inverse
        hat_dot = gain * (signal_dot * inverse - signal * (inverse * inverse * inverse * inner))
        return hat.astype(BF16), hat_dot.astype(BF16)

    groups = out_refs[0].shape[0]
    counts = [ref.shape[2] // (6 * HD) for ref in out_refs]
    heads = sum(counts)
    target = [(ref, j) for ref, count in zip(out_refs, counts) for j in range(count)]
    q, qd = normed(q_ref, qd_ref, gq_ref)
    k, kd = normed(k_ref, kd_ref, gk_ref)
    pieces = (qd, q, k, kd, v_ref[...], vd_ref[...])
    for g in range(groups):
        for h in range(heads):
            src = (g * heads + h) * HD
            ref, j = target[h]
            for i, piece in enumerate(pieces):
                dst = (6 * j + i) * HD
                ref[g, :, dst : dst + HD] = piece[:, src : src + HD]


def norm_pack(q, qd, k, kd, v, vd, gq, gk, groups, counts):
    tokens, width = q.shape
    rows = 64
    wide = pl.BlockSpec((rows, width), lambda i: (i, 0))
    gain = pl.BlockSpec((1, width), lambda i: (0, 0))
    return pl.pallas_call(
        norm_body,
        grid=(tokens // rows,),
        in_specs=[wide] * 6 + [gain] * 2,
        out_specs=[pl.BlockSpec((groups, rows, n * 6 * HD), lambda i: (0, i, 0)) for n in counts],
        out_shape=[jax.ShapeDtypeStruct((groups, tokens, n * 6 * HD), BF16) for n in counts],
        compiler_params=pltpu.CompilerParams(vmem_limit_bytes=VMEM_ALL),
        cost_estimate=NO_COST,
        name="norm_pack",
    )(q, qd, k, kd, v, vd, gq.reshape(1, width), gk.reshape(1, width))


NT = (((1,), (1,)), ((), ()))
NN = (((1,), (0,)), ((), ()))


def attn_body(in_ref, *refs):
    out_ref = refs[-1]
    groups, tokens, _ = in_ref.shape
    length = groups * tokens
    blocks = 8
    rows = blocks * tokens
    scale = HD**-0.5

    def columns(first, count):
        return in_ref[:, :, first * HD : (first + count) * HD].reshape(length, count * HD)

    k, kk = columns(2, 1), columns(2, 2)
    v, vv = columns(4, 1), columns(4, 2)
    for b in range(0, groups, blocks):
        both = in_ref[b : b + blocks, :, 0 : 2 * HD].reshape(rows, 2 * HD)
        q = in_ref[b : b + blocks, :, HD : 2 * HD].reshape(rows, HD)
        s = lax.dot_general(q, k, NT, preferred_element_type=F32)
        sd = lax.dot_general(both, kk, NT, preferred_element_type=F32)
        peak = jnp.max(s, axis=-1, keepdims=True)
        w = jnp.exp2((s - peak) * (scale * math.log2(math.e)))
        inv = 1.0 / jnp.sum(w, axis=-1, keepdims=True)
        mean = jnp.sum(w * sd, axis=-1, keepdims=True) * inv
        w_dot = (w * (sd - mean)).astype(BF16)
        first = lax.dot_general(w.astype(BF16), vv, NN, preferred_element_type=F32)
        second = lax.dot_general(w_dot, v, NN, preferred_element_type=F32)
        attn = (first[:, :HD] * inv).astype(BF16)
        attn_dot = ((second * scale + first[:, HD:]) * inv).astype(BF16)
        out_ref[b : b + blocks, :, 0:HD] = attn.reshape(blocks, tokens, HD)
        out_ref[b : b + blocks, :, HD : 2 * HD] = attn_dot.reshape(blocks, tokens, HD)


def attend(packed, first, heads, earlier=None):
    groups, tokens, width = packed.shape
    return pl.pallas_call(
        attn_body,
        grid=(width // (6 * HD),),
        in_specs=[pl.BlockSpec((groups, tokens, 6 * HD), lambda h: (0, 0, h))]
        + ([] if earlier is None else [pl.BlockSpec(memory_space=pl.ANY)]),
        out_specs=pl.BlockSpec((groups, tokens, 2 * HD), lambda h: (0, 0, first + h)),
        out_shape=jax.ShapeDtypeStruct((groups, tokens, heads * 2 * HD), BF16),
        input_output_aliases={} if earlier is None else {1: 0},
        compiler_params=pltpu.CompilerParams(vmem_limit_bytes=VMEM_ALL - 3 * MIB // 2),
        cost_estimate=NO_COST,
        name="attend",
    )(packed, *(() if earlier is None else (earlier,)))


def prepare_body(n, times_ref, info_ref, gate_hbm, gate_dot_hbm, *rest):
    weights = rest[:n]
    gates_ref, w_ref, wide, sem, w_sem = rest[n:]
    copies, at = [], 0
    for who in range(2):
        row = pl.multiple_of(times_ref[who] // 8 * 8, 8)
        for t, table in enumerate((gate_hbm, gate_dot_hbm)):
            copies.append(pltpu.make_async_copy(table.at[pl.ds(row, 8), :], wide.at[who, t], sem.at[who, t]))
    for i, weight in enumerate(weights):
        rows = weight.shape[0]
        copies.append(pltpu.make_async_copy(weight, w_ref.at[pl.ds(at, rows), :], w_sem.at[i]))
        at += rows
    for c in copies:
        c.start()
    for c in copies:
        c.wait()
    for who in range(2):
        row = times_ref[who] % 8
        for t in range(2):
            parts = []
            for i in range(gates_ref.shape[1] // PIECE):
                column = info_ref[i] * PIECE
                base = pl.multiple_of(column // HD * HD, HD)
                line = wide[who, t, pl.ds(row, 1), pl.ds(base, 3 * HD)]
                parts.append(jnp.where(column % HD != 0, line[:, HD // 2 : HD // 2 + PIECE], line[:, :PIECE]))
            gates_ref[2 * who + t : 2 * who + t + 1] = jnp.concatenate(parts, axis=1)


def prepare(times, info, gate_table, gate_dot_table, weights):
    width = gate_table.shape[1]
    n = len(weights)
    total = sum(a.shape[0] for a in weights)
    anywhere = pl.BlockSpec(memory_space=pl.ANY)
    depth = weights[0].shape[1]
    return pl.pallas_call(
        functools.partial(prepare_body, n),
        grid=(1,),
        in_specs=[pl.BlockSpec(memory_space=pltpu.SMEM)] * 2 + [anywhere] * (2 + n),
        out_specs=[pl.BlockSpec((8, 8 * PIECE), lambda i: (0, 0)), pl.BlockSpec((total, depth), lambda i: (0, 0))],
        out_shape=[
            jax.ShapeDtypeStruct((2048, 8 * PIECE), F32),
            jax.ShapeDtypeStruct((total, weights[0].shape[1]), BF16),
        ],
        scratch_shapes=[
            pltpu.VMEM((2, 2, 8, width), F32),
            pltpu.SemaphoreType.DMA((2, 2)),
            pltpu.SemaphoreType.DMA((n,)),
        ],
        compiler_params=pltpu.CompilerParams(vmem_limit_bytes=VMEM_ALL),
        cost_estimate=NO_COST,
        name="prepare",
    )(times, info, gate_table, gate_dot_table, *weights)


def round_up(n, unit):
    return -(-n // unit) * unit


def project_body(n, first, ready_rows, plan, gates_any, own_ref, peer_ref, *rest):
    ready = rest[0] if ready_rows else None
    rest = rest[1:] if ready_rows else rest
    weights = rest[:n]
    mine_ref, send_ref, x, w, gates_own, w_sem, g_sem = rest[n:]
    groups, tokens, _ = own_ref.shape
    heads = own_ref.shape[2] // (2 * HD)

    gates_ref = gates_any if ready_rows else gates_own
    at, w_copies = 0, []
    for i, (which, start, rows) in enumerate(plan):
        piece = weights[which].at[pl.ds(start, rows), :]
        w_copies.append(pltpu.make_async_copy(piece, w.at[pl.ds(at, rows), :], w_sem.at[i]))
        at += rows
    for c in w_copies:
        c.start()
    gates_copy = None
    if not ready_rows:
        gates_copy = pltpu.make_async_copy(gates_any.at[pl.ds(0, 8), :], gates_own, g_sem)
        gates_copy.start()

    for who, ref in enumerate((own_ref, peer_ref)):
        for g in range(groups):
            for h in range(heads):
                at = (g * heads + h) * HD
                for t in range(2):
                    row = (2 * who + t) * tokens
                    src = (2 * h + t) * HD
                    x[row : row + tokens, at : at + HD] = ref[g, :, src : src + HD]

    def part(weight_ref, begin):
        end = begin + weight_ref.shape[0]
        y = lax.dot_general(x[...], weight_ref[...], NT, preferred_element_type=F32)
        for who, ref in enumerate((mine_ref, send_ref)):
            lines = slice(first * PIECE + begin, first * PIECE + end)
            gate, gate_dot = (gates_ref[2 * who + t : 2 * who + t + 1, lines] for t in range(2))
            primal = y[2 * who * tokens : (2 * who + 1) * tokens]
            tangent = y[(2 * who + 1) * tokens : (2 * who + 2) * tokens]
            ref[0, :, begin:end] = (gate * primal).astype(BF16)
            ref[1, :, begin:end] = (gate_dot * primal + gate * tangent).astype(BF16)

    if ready_rows:
        part(ready, 0)
    else:
        gates_copy.wait()
    for c in w_copies:
        c.wait()
    part(w, ready_rows)


def whole(a):
    return pl.BlockSpec(a.shape, lambda i: (0,) * len(a.shape))


def project(first, own, peer, gates, ready, weights, plan=None):
    groups, tokens, _ = own.shape
    n = len(weights)
    plan = plan or [(i, 0, a.shape[0]) for i, a in enumerate(weights)]
    rows = sum(count for _, _, count in plan)
    ready_rows = 0 if ready is None else ready.shape[0]
    depth = weights[0].shape[1]
    hbm = pl.BlockSpec(memory_space=pltpu.HBM)
    half = jax.ShapeDtypeStruct((2, tokens, round_up(ready_rows + rows, HD)), BF16)
    return pl.pallas_call(
        functools.partial(project_body, n, first, ready_rows, plan),
        grid=(1,),
        in_specs=[hbm if ready is None else pl.BlockSpec((8, gates.shape[1]), lambda i: (0, 0))]
        + [whole(a) for a in ((own, peer) if ready is None else (own, peer, ready))]
        + [hbm] * n,
        out_specs=[whole(half), whole(half)],
        out_shape=[half, half],
        scratch_shapes=[
            pltpu.VMEM((4 * tokens, depth), BF16),
            pltpu.VMEM((rows, depth), BF16),
            pltpu.VMEM((8, gates.shape[1]), F32),
            pltpu.SemaphoreType.DMA((len(plan),)),
            pltpu.SemaphoreType.DMA,
        ],
        compiler_params=pltpu.CompilerParams(vmem_limit_bytes=36 * MIB),
        cost_estimate=NO_COST,
        name="project",
    )(gates, own, peer, *(() if ready is None else (ready,)), *weights)


def merge_body(spots, info_ref, *refs):
    parts = (len(refs) - 4) // 2
    out_hbm = refs[2 * parts : 2 * parts + 2]
    outs, sem = refs[2 * parts + 2 :]
    first = info_ref[8] == 0
    copies = []
    for t in range(2):
        for i, (part, at) in enumerate(spots):
            own_ref, got_ref = refs[part], refs[parts + part]
            cols = 2 * PIECE
            column = pl.multiple_of(info_ref[9 + i] * cols, cols)
            here = slice(at * PIECE, (at + 1) * PIECE)
            own, got = own_ref[t, :, here], got_ref[t, :, here]
            low = jnp.where(first, own, got)
            high = jnp.where(first, got, own)
            outs[t, :, pl.ds(column, cols)] = jnp.concatenate([low, high], axis=1)
        copies.append(pltpu.make_async_copy(outs.at[t], out_hbm[t], sem.at[t]))
        copies[t].start()
    for c in copies:
        c.wait()


def merge(info, spots, owns, gots, width):
    tokens = owns[0].shape[1]
    vmem = pl.BlockSpec(memory_space=pltpu.VMEM)
    anywhere = pl.BlockSpec(memory_space=pl.ANY)
    out = jax.ShapeDtypeStruct((tokens, width), BF16)
    return pl.pallas_call(
        functools.partial(merge_body, spots),
        in_specs=[pl.BlockSpec(memory_space=pltpu.SMEM)] + [vmem] * (2 * len(owns)),
        out_specs=[anywhere, anywhere],
        out_shape=[out, out],
        scratch_shapes=[pltpu.VMEM((2, tokens, width), BF16), pltpu.SemaphoreType.DMA((2,))],
        compiler_params=pltpu.CompilerParams(vmem_limit_bytes=12 * MIB),
        cost_estimate=NO_COST,
        name="merge",
    )(info, *owns, *gots)


def local(
    query_raw,
    key_raw,
    value_in,
    query_dot,
    key_dot,
    value_dot,
    gain_query,
    gain_key,
    out_weight,
    gate_table,
    gate_dot_table,
    time_index,
):
    groups = lax.axis_size("seq")
    fsdp = lax.axis_index("fsdp")
    core = fsdp % NC
    x_lo = fsdp // NC % NXL
    y = fsdp // (NC * NXL)
    up, down, swap = along_y(1), along_y(-1), core_swap()

    def exchange(a):
        return lax.all_to_all(a, "seq", split_axis=0, concat_axis=0, tiled=True)

    other = 1 - x_lo
    steps = (0, -1, 1, 2)
    block = [(y + step) % NY * NXL + low for low in (x_lo, other) for step in steps]
    source = [index * NC + core for index in block]
    info = jnp.stack([jnp.asarray(v, jnp.int32) for v in (*source, core, *block)])

    weight = out_weight.T
    early = 160
    near = move(weight, beside())
    w1 = weight[:early]
    a1 = move(w1, up)
    b1 = move(w1, down)
    peer_time = move(time_index, swap)
    (packed,) = norm_pack(
        query_raw, query_dot, key_raw, key_dot, value_in, value_dot, gain_query, gain_key, groups, (3,)
    )
    times = jnp.concatenate([time_index, peer_time])
    packed, weight, near, a1, b1, times, info = lax.optimization_barrier(
        (packed, weight, near, a1, b1, times, info)
    )

    received = exchange(packed)
    w2 = weight[early:]
    a2 = move(w2, up)
    b2 = move(w2, down)
    c1 = move(a1, up)
    c2 = move(b2, down)
    quarter = PIECE // 4
    near_a1 = move(near[:quarter], up)
    near_a2 = move(near[quarter:], up)
    near_b1 = move(near[quarter:early], down)
    near_b2 = move(jnp.concatenate([near[:quarter], near[early:]]), down)
    received, a2, b2, c1, c2 = lax.optimization_barrier((received, a2, b2, c1, c2))

    attn = attend(received, 0, 3)
    own = exchange(attn)
    gates, here = prepare(times, info, gate_table, gate_dot_table, (weight, a1, a2, b1, b2, c1, c2))
    own, near_a2, near_b2, gates, here, c2 = lax.optimization_barrier((own, near_a2, near_b2, gates, here, c2))
    own, near_a1, near_b1 = lax.optimization_barrier((own, near_a1, near_b1))

    peer = move(own, swap)
    near_c1 = move(near_a1, up)
    near_c2 = move(near_b1, down)
    near_c3 = move(c2, beside())

    mine_a, sent_a = project(
        0,
        own,
        peer,
        gates,
        here,
        (near, near_a1, near_a2, near_b1, near_b2),
        [(0, 0, PIECE), (1, 0, quarter), (2, 0, PIECE - quarter), (4, 0, quarter), (3, 0, early - quarter), (4, quarter, PIECE - early)],
    )
    mine_a, sent_a, near_c1, near_c2, near_c3 = lax.optimization_barrier((mine_a, sent_a, near_c1, near_c2, near_c3))
    got_a = move(sent_a, swap)
    mine_b, sent_b = project(7, own, peer, gates, None, (near_c1, near_c2, near_c3))
    got_b = move(sent_b, swap)
    spots = [(0, i) for i in range(7)] + [(1, 0)]
    return tuple(merge(info, spots, (mine_a, mine_b), (got_a, got_b), gate_table.shape[1]))


def solution(mesh):
    return jax.shard_map(
        local,
        mesh=mesh,
        in_specs=(
            P(("fsdp", "seq"), None),
            P(("fsdp", "seq"), None),
            P(("fsdp", "seq"), None),
            P(("fsdp", "seq"), None),
            P(("fsdp", "seq"), None),
            P(("fsdp", "seq"), None),
            P(),
            P(),
            P(None, "fsdp"),
            P(),
            P(),
            P("fsdp"),
        ),
        out_specs=(P(("fsdp", "seq"), None), P(("fsdp", "seq"), None)),
        check_vma=False,
    )
```
